32 devices in a mesh: sta: 8 (over z, y), seg: 4 (over x, core).
Axes of the slice: x: 2, y: 2, z: 4, core: 2. Of those that a mesh axis runs over, the one named last changes fastest.
Arguments:
- records: bfloat16 [128, 8192], P('sta', 'seg'), may hold values from -300 to 300, as said below
- owners: int32 [64, 4], P('sta'), may hold values from 0 to 7, all different within a row; in each aligned block of 8 rows (0 to 7, 8 to 15, ...) at most 8 rows name the same one
Outputs:
- whitened: bfloat16 [128, 8192], P('sta', 'seg')
- correlations: bfloat16 [128, 128, 512], P('seg', 'sta')
The draws below stay inside these ranges and needn't reach their ends.
Inputs may be any that keep to these rules, and one draw needn't show every extreme that they name: Each row names 4 different owners; among the 8 blocks of one index of sta no owner is named more than 8 times, some owner is named exactly 8 times, and every owner is named by some block. Real-valued records.
All inputs are finite; a program needn't handle non-finite values.
Results may differ from the reference program's by a relative error of at most 0.017.
Values may be sent and summed in bfloat16 or wider, within the bound.
A program may use at most 128 MiB of HBM per device.

```python
import math
import jax
import jax.numpy as jnp
import numpy as np
from jax import lax

STA_DEV = 16
SEG = 2048
LAGS = 512
BS = 2
DESTS = 4
BPD = 8
CAP = 8
R = 128
S = 128
NBLK = 64
WINDOW = 8192
N_STA = 8
N_SEG = 4


def draw_records(key, part):
    key_list = jax.random.split(key, 4)
    array_shape = (S, WINDOW)
    noise_base = jnp.clip(jax.random.normal(key_list[0], array_shape, jnp.float32), -5.0, 5.0)
    station_gain = jnp.exp(jax.random.uniform(key_list[2], (S, 1), jnp.float32, 0.0, math.log(10.0)))
    piece_gain = jnp.exp(jax.random.uniform(key_list[3], (S, WINDOW // 64), jnp.float32, math.log(0.5), math.log(2.0)))
    piece_gain = jnp.repeat(piece_gain, 64, axis=1)
    time_ramp = jnp.exp(math.log(3.0) * jnp.arange(WINDOW, dtype=jnp.float32) / WINDOW)
    return (noise_base * station_gain * piece_gain * time_ramp[None, :]).astype(jnp.bfloat16)


def assign_block(own_key, own, number, rows, amount, top, limit, lean):
    order = jax.random.permutation(own_key, amount)
    crowded, ordinary = portions_of(amount, rows * top, limit, lean, True), portions_of(amount, rows * top, limit, lean, False)
    places = jnp.arange(amount)

    def named(tallies, offset_by):
        used = int((tallies > 0).sum())
        fixed = max(1, used // 4)
        shifted = fixed + (places - fixed + offset_by * (used - fixed)) % max(1, amount - fixed)
        return jnp.zeros((amount,), jnp.int32).at[order[jnp.where(places < fixed, places, shifted)]].set(jnp.asarray(tallies, jnp.int32))

    tallies = jnp.where(number % 4 == 0, named(crowded, number // 4), named(ordinary, number - number // 4 - 1))
    mixed = jax.random.permutation(jax.random.fold_in(own, 3), amount)
    source_of, taker = mixed[0:amount // 2 * 2:2], mixed[1:amount // 2 * 2:2]
    slack = jnp.minimum(tallies[source_of] - 1, limit - tallies[taker]) // 2
    slack = jnp.where((source_of == order[0]) | (taker == order[0]) | (tallies[taker] == 0), 0, jnp.maximum(slack, 0))
    shifted = jax.random.randint(jax.random.fold_in(own, 4), (amount // 2,), 0, 1 << 20) % (slack + 1)
    tallies = tallies.at[source_of].add(-shifted).at[taker].add(shifted)
    items = jnp.searchsorted(jnp.cumsum(tallies), jnp.arange(rows * top), side="right").astype(jnp.int32)
    grid = items.reshape(top, rows).T
    grid = grid[jax.random.permutation(jax.random.fold_in(own, 1), rows)]
    offset_by = jax.random.randint(jax.random.fold_in(own, 2), (rows, 1), 0, top)
    return jnp.take_along_axis(grid, (jnp.arange(top)[None, :] + offset_by) % top, axis=1)


def portions_of(count, total, limit, skew, full):
    weights = [(1 << 20) // math.isqrt(rank ** skew) + 1 for rank in range(1, count + 1)]
    largest = limit if full else min(limit, max(-(-total // count), total * weights[0] // sum(weights)))
    least = 1 if total - largest >= count - 1 else 0
    holding, spare = [largest] + [least] * (count - 1), total - largest - least * (count - 1)
    while spare > 0:
        movable = [i for i in range(1, count) if holding[i] < largest] or [i for i in range(1, count) if holding[i] < limit]
        pool, budget = sum([weights[i] for i in movable]), spare
        for i in movable:
            addition = min(limit - holding[i], max(1, budget * weights[i] // pool), spare)
            holding[i] = holding[i] + addition
            spare = spare - addition
    return np.array(holding)


def setup_inputs(seed: int = 0) -> dict:
    streams_of = jax.random.split(jax.random.key(seed), 3)
    records = draw_records(jax.random.fold_in(streams_of[2], 71), 0)
    owners_keys = jax.random.split(jax.random.fold_in(streams_of[1], 1), NBLK // BPD)
    owners_turns = jax.random.permutation(jax.random.fold_in(streams_of[1], 3), NBLK // BPD)
    owners = jax.vmap(lambda own, number: assign_block(jax.random.fold_in(streams_of[1], 2), own, number, BPD, N_STA, DESTS, CAP, 2))(owners_keys, owners_turns).reshape((NBLK, DESTS))
    return {"records": records, "owners": owners}


WATER = 0.5
EPSILON = 1e-06

def make_table(length):
    sample_ids = jnp.arange(length, dtype=jnp.int32)
    product = sample_ids[:, None] * sample_ids[None, :] % length
    angles = product.astype(jnp.float32) * (2.0 * math.pi / length)
    return jnp.concatenate([jnp.cos(angles), jnp.sin(angles)], axis=1).astype(jnp.bfloat16)

def reference(records, owners):
    dft_table = make_table(SEG)
    seg_rows = records.reshape(S * N_SEG, SEG)
    spectrum = jnp.dot(seg_rows, dft_table, preferred_element_type=jnp.float32)
    real_part = spectrum[:, :SEG]
    imag_part = spectrum[:, SEG:]
    magnitude = jnp.sqrt(real_part * real_part + imag_part * imag_part)
    amp_total = lax.optimization_barrier(jnp.sum(magnitude.reshape(S, N_SEG * SEG), axis=1))
    water_level = WATER * amp_total / WINDOW + EPSILON
    level_rows = jnp.repeat(water_level, N_SEG)[:, None]
    flattened = (spectrum / (jnp.concatenate([magnitude, magnitude], axis=1) + level_rows)).astype(jnp.bfloat16)
    white_trace = lax.dot_general(flattened, dft_table, (((1,), (1,)), ((), ())), preferred_element_type=jnp.float32) * (1.0 / SEG)
    white_trace = white_trace.reshape(S, WINDOW)
    energy = lax.optimization_barrier(jnp.sum(white_trace * white_trace, axis=1))
    whitened = (white_trace * lax.rsqrt(energy / WINDOW + EPSILON)[:, None]).astype(jnp.bfloat16)
    series = whitened.astype(jnp.float32)
    half_lags = LAGS // 2
    fft_len = 1 << (SEG + LAGS - 1).bit_length()
    padded_series = jnp.pad(series, ((0, 0), (half_lags, half_lags)))
    window_index = (np.arange(N_SEG) * SEG)[:, None] + np.arange(SEG + LAGS)[None, :]
    own_windows = padded_series[:, window_index]
    own_spectra = jnp.fft.rfft(own_windows, n=fft_len, axis=-1)
    seg_spectra = jnp.fft.rfft(series.reshape(S, N_SEG, SEG), n=fft_len, axis=-1)
    spec_real = jnp.real(seg_spectra).reshape(N_STA, BPD, BS, N_SEG, -1)
    spec_imag = jnp.imag(seg_spectra).reshape(N_STA, BPD, BS, N_SEG, -1)
    owner_ids = jnp.arange(N_STA, dtype=jnp.int32)
    wanted = jnp.any(owners[:, :, None] == owner_ids[None, None, :], axis=1).reshape(N_STA, BPD, N_STA)
    wanted_count = wanted.astype(jnp.int32)
    slot_rank = jnp.cumsum(wanted_count, axis=1) - wanted_count
    slot_ids = jnp.arange(CAP, dtype=jnp.int32)
    lag_index = np.arange(LAGS, 0, -1)
    corr_scale = 1.0 / math.sqrt(WINDOW)

    def one_owner(owner):
        chosen = wanted[:, :, owner]
        ranks = slot_rank[:, :, owner]
        selector = (chosen[:, None, :] & (ranks[:, None, :] == slot_ids[None, :, None])).astype(jnp.float32)
        recv_real = jnp.einsum('sqj,sjbgf->sqbgf', selector, spec_real, precision=lax.Precision.HIGHEST).reshape(R, N_SEG, -1)
        recv_imag = jnp.einsum('sqj,sjbgf->sqbgf', selector, spec_imag, precision=lax.Precision.HIGHEST).reshape(R, N_SEG, -1)
        own_part = lax.dynamic_slice_in_dim(own_spectra, owner * STA_DEV, STA_DEV, 0)

        def one_segment(carry, seg_id):
            real_seg = lax.dynamic_index_in_dim(recv_real, seg_id, 1, False)
            imag_seg = lax.dynamic_index_in_dim(recv_imag, seg_id, 1, False)
            conj_recv = real_seg - 1j * imag_seg
            own_seg = lax.dynamic_index_in_dim(own_part, seg_id, 1, False)
            cross = conj_recv[:, None, :] * own_seg[None, :, :]
            lagged = jnp.fft.irfft(cross, n=fft_len, axis=-1)[:, :, lag_index] * corr_scale
            rounded = lax.optimization_barrier(lagged.astype(jnp.bfloat16)).astype(jnp.float32)
            return (carry + rounded, None)
        summed, unused = lax.scan(one_segment, jnp.zeros((R, STA_DEV, LAGS), jnp.float32), jnp.arange(N_SEG, dtype=jnp.int32))
        return summed.astype(jnp.bfloat16)
    per_owner = lax.map(one_owner, owner_ids)
    correlations = jnp.transpose(per_owner, (1, 0, 2, 3)).reshape(R, S, LAGS)
    return (whitened, correlations)
```

```python
import functools
import math

import jax
import jax.numpy as jnp
import numpy as np
from jax import lax
from jax.experimental import pallas as pl
from jax.experimental.pallas import tpu as pltpu
from jax.sharding import PartitionSpec as P

LAGS = 512
LANES = 128
BS = 2
DESTS = 4
SUB = 32

WATER = 0.5
EPSILON = 1e-06
MESH = pl.DeviceIdType.MESH


def conj(value):
    return value[0], -value[1]


def real_dft(slabs):
    n = len(slabs)
    if n == 2:
        zero = jnp.zeros_like(slabs[0])
        return [(slabs[0] + slabs[1], zero), (slabs[0] - slabs[1], zero)]
    even, odd = real_dft(slabs[::2]), real_dft(slabs[1::2])
    half = n // 2

    def at(values, k):
        k %= half
        return values[k] if k <= half // 2 else conj(values[half - k])

    result = []
    for k in range(half + 1):
        c, s = math.cos(2 * math.pi * k / n), math.sin(2 * math.pi * k / n)
        (er, ei), (pr, pi) = at(even, k), at(odd, k)
        if k == 0:
            result.append((er + pr, ei + pi))
        elif k == half:
            result.append((er - pr, ei - pi))
        elif 4 * k == n:
            result.append((er - pi, ei + pr))
        else:
            result.append((er + c * pr - s * pi, ei + s * pr + c * pi))
    return result


def real_inverse(values, n):
    if n == 2:
        return [values[0][0] + values[1][0], values[0][0] - values[1][0]]
    half = n // 2
    even, odd = [], []
    for k in range(half // 2 + 1):
        (ar, ai), (br, bi) = values[k], conj(values[half - k])
        even.append((ar + br, ai + bi))
        dr, di = ar - br, ai - bi
        c, s = math.cos(2 * math.pi * k / n), math.sin(2 * math.pi * k / n)
        if k == 0:
            odd.append((dr, di))
        elif 4 * k == n:
            odd.append((di, -dr))
        else:
            odd.append((dr * c + di * s, di * c - dr * s))
    slabs = [None] * n
    slabs[::2] = real_inverse(even, half)
    slabs[1::2] = real_inverse(odd, half)
    return slabs


def tables(seg_len):
    lanes = np.arange(LANES)
    angle = 2 * np.pi * (np.outer(lanes, lanes) % LANES) / LANES
    c, s = np.cos(angle), np.sin(angle)
    forward = np.block([[c, s], [-s, c]])
    count = seg_len // LANES // 2 + 1
    turn = 2 * np.pi * np.outer(np.arange(count), lanes) / seg_len
    twiddle = np.stack([np.cos(turn), np.sin(turn)]).astype(np.float32)
    return (
        jnp.asarray(twiddle),
        jnp.asarray(forward, jnp.bfloat16),
        jnp.asarray(forward.T, jnp.bfloat16),
    )


def whiten(slabs, seg_count, own_count, twiddle, forward, backward):
    n1 = len(slabs)
    seg_len = n1 * LANES
    window = seg_len * seg_count
    rows = seg_count * own_count

    def over_window(value):
        total = value[:own_count]
        for g in range(1, seg_count):
            total = total + value[g * own_count : (g + 1) * own_count]
        return jnp.sum(total, axis=1, keepdims=True)

    def every_segment(value):
        return jnp.concatenate([value] * seg_count, axis=0)

    first = real_dft(slabs)
    turned = []
    for k, (re, im) in enumerate(first):
        if k:
            c, s = twiddle[0, k : k + 1, :], twiddle[1, k : k + 1, :]
            re, im = re * c - im * s, re * s + im * c
        turned.append(jnp.concatenate([re, im], axis=1).astype(jnp.bfloat16))
    spectrum = jnp.dot(
        jnp.concatenate(turned, axis=0), forward, preferred_element_type=jnp.float32
    )
    parts, total = [], None
    for k in range(len(first)):
        re = spectrum[k * rows : (k + 1) * rows, :LANES]
        im = spectrum[k * rows : (k + 1) * rows, LANES:]
        magnitude = jnp.sqrt(re * re + im * im)
        parts.append((re, im, magnitude))
        term = magnitude if k in (0, n1 // 2) else 2.0 * magnitude
        total = term if total is None else total + term
    level = every_segment(WATER * over_window(total) / window + EPSILON)
    flat = []
    for re, im, magnitude in parts:
        inverse = 1.0 / (magnitude + level)
        flat.append(jnp.concatenate([re * inverse, im * inverse], axis=1).astype(jnp.bfloat16))
    back = jnp.dot(
        jnp.concatenate(flat, axis=0), backward, preferred_element_type=jnp.float32
    )
    turned = []
    for k in range(len(first)):
        re = back[k * rows : (k + 1) * rows, :LANES]
        im = back[k * rows : (k + 1) * rows, LANES:]
        if k:
            c, s = twiddle[0, k : k + 1, :], twiddle[1, k : k + 1, :]
            re, im = re * c + im * s, im * c - re * s
        turned.append((re, im))
    trace = [slab * (1.0 / seg_len) for slab in real_inverse(turned, n1)]
    squares = trace[0] * trace[0]
    for slab in trace[1:]:
        squares = squares + slab * slab
    scale = every_segment(lax.rsqrt(over_window(squares) / window + EPSILON))
    return [slab * scale for slab in trace]


def gather_kernel(
    n_sta,
    n_seg,
    records,
    owners,
    twiddle,
    forward,
    backward,
    white,
    own,
    received,
    held,
    seg_send,
    seg_recv,
    z_send,
    z_recv,
    y_send,
    y_recv,
):
    depth = n_sta // n_seg
    planes = n_seg
    own_count, seg_len = records.shape
    n1 = seg_len // LANES
    g, s = lax.axis_index("seg"), lax.axis_index("sta")
    z, y = s // depth, s % depth

    barrier = pltpu.get_barrier_semaphore()
    for d in range(1, n_seg):
        pl.semaphore_signal(barrier, inc=1, device_id={"seg": (g + d) % n_seg}, device_id_type=MESH)
    for d in range(1, depth):
        pl.semaphore_signal(
            barrier, inc=1, device_id={"sta": z * depth + (y + d) % depth}, device_id_type=MESH
        )

    @pl.when(z > 0)
    def _():
        pl.semaphore_signal(barrier, inc=1, device_id={"sta": s - depth}, device_id_type=MESH)

    @pl.when(z < planes - 1)
    def _():
        pl.semaphore_signal(barrier, inc=1, device_id={"sta": s + depth}, device_id_type=MESH)

    below, above = (z + planes - 1) // planes, (2 * planes - 2 - z) // planes
    pl.semaphore_wait(barrier, n_seg - 1 + depth - 1 + below + above)

    copies = []
    for d in range(1, n_seg):
        copy = pltpu.make_async_remote_copy(
            src_ref=records,
            dst_ref=held.at[g],
            send_sem=seg_send.at[d - 1],
            recv_sem=seg_recv.at[d - 1],
            device_id={"seg": (g + d) % n_seg},
            device_id_type=MESH,
        )
        copy.start()
        copies.append(copy)
    held[g] = records[...]
    for copy in copies:
        copy.wait()

    slabs = []
    for t in range(n1):
        slabs.append(
            jnp.concatenate(
                [held[j, :, t * LANES : (t + 1) * LANES].astype(jnp.float32) for j in range(n_seg)],
                axis=0,
            )
        )
    result = whiten(slabs, n_seg, own_count, twiddle, forward[...], backward[...])
    for t in range(n1):
        rounded = result[t].astype(jnp.bfloat16)
        for j in range(n_seg):
            own[j * n1 + t] = rounded[j * own_count : (j + 1) * own_count]
    own[n_seg * n1] = owners[...]

    @pl.when(z == g)
    def _():
        received[y] = own[...]

    up = jnp.logical_and(z >= g, z < planes - 1)
    down = jnp.logical_and(z <= g, z > 0)

    def along_z(j, target):
        size = n1 + (1 if j == n_seg - 1 else 0)
        part = received.at[y, pl.ds(j * n1, size)]
        return pltpu.make_async_remote_copy(
            src_ref=part,
            dst_ref=part,
            send_sem=z_send.at[j],
            recv_sem=z_recv.at[j],
            device_id={"sta": target},
            device_id_type=MESH,
        )

    def along_z_up(j):
        return along_z(j, s + depth)

    def along_z_down(j):
        size = n1 + (1 if j == n_seg - 1 else 0)
        part = received.at[y, pl.ds(j * n1, size)]
        return pltpu.make_async_remote_copy(
            src_ref=part,
            dst_ref=part,
            send_sem=z_send.at[n_seg + j],
            recv_sem=z_recv.at[j],
            device_id={"sta": s - depth},
            device_id_type=MESH,
        )

    def along_y(j, d):
        size = n1 + (1 if j == n_seg - 1 else 0)
        part = received.at[y, pl.ds(j * n1, size)]
        return pltpu.make_async_remote_copy(
            src_ref=part,
            dst_ref=part,
            send_sem=y_send.at[d - 1, j],
            recv_sem=y_recv.at[d - 1, j],
            device_id={"sta": z * depth + (y + d) % depth},
            device_id_type=MESH,
        )

    for j in range(n_seg):

        @pl.when(z != g)
        def _():
            along_z_up(j).wait_recv()

        @pl.when(up)
        def _():
            along_z_up(j).start()

        @pl.when(down)
        def _():
            along_z_down(j).start()

        for d in range(1, depth):
            along_y(j, d).start()
    for t in range(n1):
        white[:, t * LANES : (t + 1) * LANES] = own[g * n1 + t]
    for j in range(n_seg):
        for d in range(1, depth):
            along_y(j, d).wait()

        @pl.when(up)
        def _():
            along_z_up(j).wait_send()

        @pl.when(down)
        def _():
            along_z_down(j).wait_send()


def lag_kernel(n_sta, n_seg, slots, own, received, flip, out, ext, rec, left, sums):
    depth = n_sta // n_seg
    nk, own_count = own.shape[0] - 1, own.shape[1]
    stations = depth * own_count
    parts = LANES // SUB
    tiles = LAGS // LANES + 1
    edge = LAGS // 2 // LANES
    me = lax.axis_index("sta").astype(jnp.float32)
    lane = lax.broadcasted_iota(jnp.int32, (own_count, LANES), 1)

    zero = jnp.zeros((own_count, LANES), jnp.float32)

    def padded(k):
        inside = 0 <= k - edge < nk
        return own[k - edge].astype(jnp.float32) if inside else zero

    def spread(k, now, later):
        ext[0, k] = now
        for c in range(1, parts):
            shift = LANES - SUB * c
            ext[c, k] = jnp.where(
                lane < shift, pltpu.roll(now, shift, 1), pltpu.roll(later, shift, 1)
            )

    for k in list(range(edge)) + list(range(nk + edge - 1, nk + tiles - 1)):
        spread(k, padded(k), padded(k + 1))

    def inner(k, carry):
        spread(k, own[k - edge].astype(jnp.float32), own[k - edge + 1].astype(jnp.float32))
        return carry

    lax.fori_loop(edge, nk + edge - 1, inner, 0)

    for y in range(depth):
        rec[...] = received[y, :nk].astype(jnp.float32)
        for b in range(own_count):
            turned = rec[:, b, :].T
            for c in range(parts):
                left[:, y * own_count + b, c * nk : (c + 1) * nk] = turned[
                    c * SUB : (c + 1) * SUB
                ]
    lhs = left[...].reshape(SUB * stations, parts * nk).astype(jnp.bfloat16)

    shape = (stations, stations)
    row = lax.broadcasted_iota(jnp.int32, shape, 0)
    station = lax.broadcasted_iota(jnp.int32, (1, stations), 1)
    source, block = station // own_count, station % own_count // BS
    number = lax.broadcasted_iota(jnp.int32, (own_count, stations), 0)
    wanted = jnp.zeros((1, stations), jnp.float32)
    rank = jnp.zeros((1, stations), jnp.float32)
    for y in range(depth):
        names = received[y, nk].astype(jnp.float32)
        named = jnp.max(
            jnp.where(jnp.logical_and(lane < DESTS, names == me), 1.0, 0.0), axis=1, keepdims=True
        )
        named = jnp.where(source == y, named, 0.0)
        wanted = wanted + jnp.sum(jnp.where(number == block, named, 0.0), axis=0, keepdims=True)
        rank = rank + jnp.sum(jnp.where(number < block, named, 0.0), axis=0, keepdims=True)
    slot = row // BS % slots
    hit = jnp.logical_and(row // (BS * slots) == source, row % BS == station % BS)
    hit = jnp.logical_and(hit, slot == rank.astype(jnp.int32))
    select = jnp.where(hit, wanted, 0.0).astype(jnp.bfloat16)
    rows = out.shape[0]
    window = nk * LANES
    scale = 1.0 / math.sqrt(window)

    for a in range(own_count):
        rhs = jnp.concatenate(
            [
                jnp.concatenate([ext[c, v : v + nk, a, :] for v in range(tiles)], axis=1)
                for c in range(parts)
            ],
            axis=0,
        ).astype(jnp.bfloat16)
        gram = jnp.dot(lhs, rhs, preferred_element_type=jnp.float32)
        terms = [gram[i * stations : (i + 1) * stations] for i in range(SUB)]
        width = tiles * LANES
        step = 1
        while len(terms) > 1:
            terms = [
                terms[i] + pltpu.roll(terms[i + 1], width - step, 1)
                for i in range(0, len(terms), 2)
            ]
            step *= 2
        total = pltpu.roll(terms[0], width - 1, 1)[:, :LAGS] * scale
        sums[a] = jnp.dot(
            select, total.astype(jnp.bfloat16), preferred_element_type=jnp.float32
        ).astype(jnp.bfloat16)[:rows]
    for a in range(own_count):
        out[:, a, :] = jnp.dot(
            sums[a], flip[...], preferred_element_type=jnp.float32
        ).astype(jnp.bfloat16)


def on_device(n_sta, n_seg, records, owners):
    own_count, seg_len = records.shape
    depth = n_sta // n_seg
    n1 = seg_len // LANES
    nk = n1 * n_seg
    blocks = own_count // BS
    slots = max(2, 2 * blocks * DESTS // n_sta)
    names = jnp.pad(
        owners.astype(jnp.bfloat16), ((0, own_count - blocks), (0, LANES - DESTS))
    )
    vmem = pl.BlockSpec(memory_space=pltpu.VMEM)
    white, own, received = pl.pallas_call(
        functools.partial(gather_kernel, n_sta, n_seg),
        out_shape=(
            jax.ShapeDtypeStruct((own_count, seg_len), jnp.bfloat16),
            jax.ShapeDtypeStruct((nk + 1, own_count, LANES), jnp.bfloat16),
            jax.ShapeDtypeStruct((depth, nk + 1, own_count, LANES), jnp.bfloat16),
        ),
        in_specs=[vmem] * 5,
        out_specs=(vmem,) * 3,
        scratch_shapes=[
            pltpu.VMEM((n_seg, own_count, seg_len), jnp.bfloat16),
            pltpu.SemaphoreType.DMA((n_seg - 1,)),
            pltpu.SemaphoreType.DMA((n_seg - 1,)),
            pltpu.SemaphoreType.DMA((2 * n_seg,)),
            pltpu.SemaphoreType.DMA((n_seg,)),
            pltpu.SemaphoreType.DMA((depth - 1, n_seg)),
            pltpu.SemaphoreType.DMA((depth - 1, n_seg)),
        ],
        compiler_params=pltpu.CompilerParams(
            collective_id=0, has_side_effects=True, vmem_limit_bytes=32 * 2**20
        ),
        name="whiten_and_gather",
    )(records, names, *tables(seg_len))
    stations = depth * own_count
    rows = depth * slots * BS
    flip = jnp.asarray(np.eye(LAGS)[::-1], jnp.bfloat16)
    parts = LANES // SUB
    tiles = LAGS // LANES + 1
    correlations = pl.pallas_call(
        functools.partial(lag_kernel, n_sta, n_seg, slots),
        out_shape=jax.ShapeDtypeStruct((rows, own_count, LAGS), jnp.bfloat16),
        in_specs=[vmem] * 3,
        out_specs=vmem,
        scratch_shapes=[
            pltpu.VMEM((parts, nk + tiles - 1, own_count, LANES), jnp.float32),
            pltpu.VMEM((nk, own_count, LANES), jnp.float32),
            pltpu.VMEM((SUB, stations, parts * nk), jnp.float32),
            pltpu.VMEM((own_count, rows, LAGS), jnp.bfloat16),
        ],
        compiler_params=pltpu.CompilerParams(vmem_limit_bytes=48 * 2**20),
        name="correlate",
    )(own, received, flip)
    return white, correlations


def solution(mesh):
    return jax.shard_map(
        functools.partial(on_device, mesh.shape["sta"], mesh.shape["seg"]),
        mesh=mesh,
        in_specs=(P("sta", "seg"), P("sta", None)),
        out_specs=(P("sta", "seg"), P("seg", "sta", None)),
        check_vma=False,
    )
```

```python
import functools
import math

import jax
import jax.numpy as jnp
import numpy as np
from jax import lax
from jax.experimental import pallas as pl
from jax.experimental.pallas import tpu as pltpu
from jax.sharding import PartitionSpec as P

LAGS = 512
LANES = 128
BS = 2
DESTS = 4
SUB = 16

WATER = 0.5
EPSILON = 1e-06
MESH = pl.DeviceIdType.MESH


def conj(value):
    return value[0], -value[1]


def real_dft(slabs):
    n = len(slabs)
    if n == 2:
        zero = jnp.zeros_like(slabs[0])
        return [(slabs[0] + slabs[1], zero), (slabs[0] - slabs[1], zero)]
    even, odd = real_dft(slabs[::2]), real_dft(slabs[1::2])
    half = n // 2

    def at(values, k):
        k %= half
        return values[k] if k <= half // 2 else conj(values[half - k])

    result = []
    for k in range(half + 1):
        c, s = math.cos(2 * math.pi * k / n), math.sin(2 * math.pi * k / n)
        (er, ei), (pr, pi) = at(even, k), at(odd, k)
        if k == 0:
            result.append((er + pr, ei + pi))
        elif k == half:
            result.append((er - pr, ei - pi))
        elif 4 * k == n:
            result.append((er - pi, ei + pr))
        else:
            result.append((er + c * pr - s * pi, ei + s * pr + c * pi))
    return result


def real_inverse(values, n):
    if n == 2:
        return [values[0][0] + values[1][0], values[0][0] - values[1][0]]
    half = n // 2
    even, odd = [], []
    for k in range(half // 2 + 1):
        (ar, ai), (br, bi) = values[k], conj(values[half - k])
        even.append((ar + br, ai + bi))
        dr, di = ar - br, ai - bi
        c, s = math.cos(2 * math.pi * k / n), math.sin(2 * math.pi * k / n)
        if k == 0:
            odd.append((dr, di))
        elif 4 * k == n:
            odd.append((di, -dr))
        else:
            odd.append((dr * c + di * s, di * c - dr * s))
    slabs = [None] * n
    slabs[::2] = real_inverse(even, half)
    slabs[1::2] = real_inverse(odd, half)
    return slabs


def tables(seg_len):
    lanes = np.arange(LANES)
    angle = 2 * np.pi * (np.outer(lanes, lanes) % LANES) / LANES
    c, s = np.cos(angle), np.sin(angle)
    forward = np.block([[c, s], [-s, c]])
    count = seg_len // LANES // 2 + 1
    turn = 2 * np.pi * np.outer(np.arange(count), lanes) / seg_len
    twiddle = np.stack([np.cos(turn), np.sin(turn)]).astype(np.float32)
    return (
        jnp.asarray(twiddle),
        jnp.asarray(forward, jnp.bfloat16),
        jnp.asarray(forward.T, jnp.bfloat16),
    )


def whiten(slabs, seg_count, own_count, twiddle, forward, backward):
    n1 = len(slabs)
    seg_len = n1 * LANES
    window = seg_len * seg_count
    rows = seg_count * own_count

    def over_window(value):
        total = value[:own_count]
        for g in range(1, seg_count):
            total = total + value[g * own_count : (g + 1) * own_count]
        return jnp.sum(total, axis=1, keepdims=True)

    def every_segment(value):
        return jnp.concatenate([value] * seg_count, axis=0)

    first = real_dft(slabs)
    turned = []
    for k, (re, im) in enumerate(first):
        if k:
            c, s = twiddle[0, k : k + 1, :], twiddle[1, k : k + 1, :]
            re, im = re * c - im * s, re * s + im * c
        turned.append(jnp.concatenate([re, im], axis=1).astype(jnp.bfloat16))
    spectrum = jnp.dot(
        jnp.concatenate(turned, axis=0), forward, preferred_element_type=jnp.float32
    )
    parts, total = [], None
    for k in range(len(first)):
        re = spectrum[k * rows : (k + 1) * rows, :LANES]
        im = spectrum[k * rows : (k + 1) * rows, LANES:]
        magnitude = jnp.sqrt(re * re + im * im)
        parts.append((re, im, magnitude))
        term = magnitude if k in (0, n1 // 2) else 2.0 * magnitude
        total = term if total is None else total + term
    level = every_segment(WATER * over_window(total) / window + EPSILON)
    flat = []
    for re, im, magnitude in parts:
        inverse = 1.0 / (magnitude + level)
        flat.append(jnp.concatenate([re * inverse, im * inverse], axis=1).astype(jnp.bfloat16))
    back = jnp.dot(
        jnp.concatenate(flat, axis=0), backward, preferred_element_type=jnp.float32
    )
    turned = []
    for k in range(len(first)):
        re = back[k * rows : (k + 1) * rows, :LANES]
        im = back[k * rows : (k + 1) * rows, LANES:]
        if k:
            c, s = twiddle[0, k : k + 1, :], twiddle[1, k : k + 1, :]
            re, im = re * c + im * s, im * c - re * s
        turned.append((re, im))
    trace = [slab * (1.0 / seg_len) for slab in real_inverse(turned, n1)]
    squares = trace[0] * trace[0]
    for slab in trace[1:]:
        squares = squares + slab * slab
    scale = every_segment(lax.rsqrt(over_window(squares) / window + EPSILON))
    return [slab * scale for slab in trace]


def gather_kernel(
    n_sta,
    n_seg,
    records,
    owners,
    twiddle_in,
    forward_in,
    backward_in,
    white,
    own,
    received,
    held,
    twiddle,
    forward,
    backward,
    names,
    table_sem,
    seg_send,
    seg_recv,
    z_send,
    z_recv,
    y_send,
    y_recv,
):
    depth = n_sta // n_seg
    planes = n_seg
    own_count, seg_len = records.shape
    n1 = seg_len // LANES
    g, s = lax.axis_index("seg"), lax.axis_index("sta")
    z, y = s // depth, s % depth

    fetches = [
        pltpu.make_async_copy(source, target, table_sem.at[i])
        for i, (source, target) in enumerate(
            (
                (records, held.at[g]),
                (twiddle_in, twiddle),
                (forward_in, forward),
                (backward_in, backward),
            )
        )
    ]
    for fetch in fetches:
        fetch.start()
    names[...] = jnp.zeros_like(names)
    names[: owners.shape[0], : owners.shape[1]] = owners[...].astype(jnp.float32)
    barrier = pltpu.get_barrier_semaphore()
    for d in range(1, n_seg):
        pl.semaphore_signal(barrier, inc=1, device_id={"seg": (g + d) % n_seg}, device_id_type=MESH)
    for d in range(1, depth):
        pl.semaphore_signal(
            barrier, inc=1, device_id={"sta": z * depth + (y + d) % depth}, device_id_type=MESH
        )

    @pl.when(z > 0)
    def _():
        pl.semaphore_signal(barrier, inc=1, device_id={"sta": s - depth}, device_id_type=MESH)

    @pl.when(z < planes - 1)
    def _():
        pl.semaphore_signal(barrier, inc=1, device_id={"sta": s + depth}, device_id_type=MESH)

    below, above = (z + planes - 1) // planes, (2 * planes - 2 - z) // planes
    pl.semaphore_wait(barrier, n_seg - 1 + depth - 1 + below + above)

    copies = []
    for d in range(1, n_seg):
        copy = pltpu.make_async_remote_copy(
            src_ref=records,
            dst_ref=held.at[g],
            send_sem=seg_send.at[d - 1],
            recv_sem=seg_recv.at[d - 1],
            device_id={"seg": (g + d) % n_seg},
            device_id_type=MESH,
        )
        copy.start()
        copies.append(copy)
    for fetch in fetches:
        fetch.wait()
    for copy in copies:
        copy.wait()

    slabs = []
    for t in range(n1):
        slabs.append(
            jnp.concatenate(
                [held[j, :, t * LANES : (t + 1) * LANES].astype(jnp.float32) for j in range(n_seg)],
                axis=0,
            )
        )
    result = whiten(slabs, n_seg, own_count, twiddle, forward[...], backward[...])
    for t in range(n1):
        rounded = result[t].astype(jnp.bfloat16)
        for j in range(n_seg):
            own[j * n1 + t] = rounded[j * own_count : (j + 1) * own_count]
    own[n_seg * n1] = names[...].astype(jnp.bfloat16)

    @pl.when(z == g)
    def _():
        received[y] = own[...]

    up = jnp.logical_and(z >= g, z < planes - 1)
    down = jnp.logical_and(z <= g, z > 0)

    def along_z(j, target):
        size = n1 + (1 if j == n_seg - 1 else 0)
        part = received.at[y, pl.ds(j * n1, size)]
        return pltpu.make_async_remote_copy(
            src_ref=part,
            dst_ref=part,
            send_sem=z_send.at[j],
            recv_sem=z_recv.at[j],
            device_id={"sta": target},
            device_id_type=MESH,
        )

    def along_z_up(j):
        return along_z(j, s + depth)

    def along_z_down(j):
        size = n1 + (1 if j == n_seg - 1 else 0)
        part = received.at[y, pl.ds(j * n1, size)]
        return pltpu.make_async_remote_copy(
            src_ref=part,
            dst_ref=part,
            send_sem=z_send.at[n_seg + j],
            recv_sem=z_recv.at[j],
            device_id={"sta": s - depth},
            device_id_type=MESH,
        )

    def along_y(j, d):
        size = n1 + (1 if j == n_seg - 1 else 0)
        part = received.at[y, pl.ds(j * n1, size)]
        return pltpu.make_async_remote_copy(
            src_ref=part,
            dst_ref=part,
            send_sem=y_send.at[d - 1, j],
            recv_sem=y_recv.at[d - 1, j],
            device_id={"sta": z * depth + (y + d) % depth},
            device_id_type=MESH,
        )

    for j in range(n_seg):

        @pl.when(z != g)
        def _():
            along_z_up(j).wait_recv()

        @pl.when(up)
        def _():
            along_z_up(j).start()

        @pl.when(down)
        def _():
            along_z_down(j).start()

        for d in range(1, depth):
            along_y(j, d).start()
    for t in range(n1):
        white[:, t * LANES : (t + 1) * LANES] = own[g * n1 + t]
    for j in range(n_seg):
        for d in range(1, depth):
            along_y(j, d).wait()

        @pl.when(up)
        def _():
            along_z_up(j).wait_send()

        @pl.when(down)
        def _():
            along_z_down(j).wait_send()


def lag_kernel(n_sta, n_seg, slots, own, received, out, flat, series, turned, rec, left, tails, sums, order):
    depth = n_sta // n_seg
    nk, own_count = own.shape[0] - 1, own.shape[1]
    stations = depth * own_count
    parts = LANES // SUB
    tiles = LAGS // LANES
    edge = LAGS // 2 // LANES
    per_tile = LANES // SUB
    me = lax.axis_index("sta").astype(jnp.float32)

    flat[...] = own[:nk].astype(jnp.float32)
    series[...] = jnp.zeros_like(series)
    for a in range(own_count):
        series[a, edge : edge + nk] = flat[:, a, :]

    for y in range(depth):
        rec[...] = received[y, :nk].astype(jnp.float32)
        for b in range(own_count):
            across = rec[:, b, :].T
            left[:, y * own_count + b, :] = jnp.concatenate(
                [across[c * SUB : (c + 1) * SUB] for c in range(parts)], axis=1
            )
    lhs = left[...].reshape(SUB * stations, parts * nk).astype(jnp.bfloat16)

    lane = lax.broadcasted_iota(jnp.int32, (nk, LANES), 1)
    for first in range(0, own_count, per_tile):
        pieces = []
        for c in range(parts):
            piece = jnp.zeros((nk, LANES), jnp.float32)
            for q in range(per_tile):
                shift = (SUB * q - SUB * c - 1) % LANES
                moved = series[first + q, tiles : tiles + nk]
                moved = pltpu.roll(moved, shift, 1) if shift else moved
                piece = jnp.where(lane // SUB == q, moved, piece)
            pieces.append(piece)
        tails[first // per_tile] = jnp.dot(
            lhs,
            jnp.concatenate(pieces, axis=0).astype(jnp.bfloat16),
            preferred_element_type=jnp.float32,
        )

    shape = (stations, stations)
    row = lax.broadcasted_iota(jnp.int32, shape, 0)
    station = lax.broadcasted_iota(jnp.int32, shape, 1)
    source, block = station // own_count, station % own_count // BS
    wide = (LANES, stations)
    number = lax.broadcasted_iota(jnp.int32, wide, 0)
    wide_station = lax.broadcasted_iota(jnp.int32, wide, 1)
    wide_block = wide_station % own_count // BS
    entry = lax.broadcasted_iota(jnp.int32, (own_count, LANES), 0)
    wanted = jnp.zeros(shape, jnp.float32)
    rank = jnp.zeros(shape, jnp.float32)
    for y in range(depth):
        names = received[y, nk].astype(jnp.float32)
        named = jnp.max(
            jnp.where(jnp.logical_and(entry < DESTS, names == me), 1.0, 0.0), axis=0, keepdims=True
        )
        named = jnp.broadcast_to(named, (stations, LANES)).astype(jnp.bfloat16)
        here = wide_station // own_count == y
        same = jnp.where(jnp.logical_and(here, number == wide_block), 1.0, 0.0)
        before = jnp.where(jnp.logical_and(here, number < wide_block), 1.0, 0.0)
        wanted += jnp.dot(named, same.astype(jnp.bfloat16), preferred_element_type=jnp.float32)
        rank += jnp.dot(named, before.astype(jnp.bfloat16), preferred_element_type=jnp.float32)
    slot = (row // BS % slots).astype(jnp.float32)
    hit = jnp.logical_and(row // (BS * slots) == source, row % BS == station % BS)
    hit = jnp.logical_and(hit, slot == rank)
    select = jnp.where(hit, wanted, 0.0).astype(jnp.bfloat16)
    rows = out.shape[0]
    window = nk * LANES
    scale = 1.0 / math.sqrt(window)
    lag_lane = lax.broadcasted_iota(jnp.int32, (stations, LANES), 1)

    def one_station(a, slot_of):
        whole = series[a]
        pieces = []
        for c in range(parts):
            shift = LANES - SUB * c - 1
            turned[slot_of, c] = pltpu.roll(whole, shift, 1)
            moved = [turned[slot_of, c, v : v + nk] for v in range(tiles + 1)]
            pieces.append(
                jnp.concatenate(
                    [jnp.where(lane < shift, moved[v], moved[v + 1]) for v in range(tiles)], axis=1
                ).astype(jnp.bfloat16)
            )
        gram = jnp.dot(lhs, jnp.concatenate(pieces, axis=0), preferred_element_type=jnp.float32)
        back = (LANES - SUB * (a % per_tile)) % LANES
        terms = []
        for i in range(SUB):
            term = gram[i * stations : (i + 1) * stations]
            if i:
                tail = tails[a // per_tile, i * stations : (i + 1) * stations]
                head = jnp.where(lag_lane < i, pltpu.roll(tail, back, 1), term[:, :LANES])
                term = jnp.concatenate([head, term[:, LANES:]], axis=1)
            terms.append(term)
        step = 1
        while len(terms) > 1:
            terms = [
                terms[i] + pltpu.roll(terms[i + 1], LAGS - step, 1)
                for i in range(0, len(terms), 2)
            ]
            step *= 2
        total = (terms[0] * scale).astype(jnp.bfloat16)
        sums[a] = jnp.dot(select, total, preferred_element_type=jnp.float32)[:rows]

    def pair(step, carry):
        one_station(2 * step, 0)
        one_station(2 * step + 1, 1)
        return carry

    lax.fori_loop(0, own_count // 2, pair, 0)
    for a in range(own_count):
        order[:, a, :] = sums[a]
    square = (LAGS, LAGS)
    ends = lax.broadcasted_iota(jnp.int32, square, 0) + lax.broadcasted_iota(jnp.int32, square, 1)
    flip = jnp.where(ends == LAGS - 1, 1.0, 0.0).astype(jnp.bfloat16)
    out[...] = (
        jnp.dot(
            order[...].reshape(rows * own_count, LAGS).astype(jnp.bfloat16),
            flip,
            preferred_element_type=jnp.float32,
        )
        .astype(jnp.bfloat16)
        .reshape(rows, own_count, LAGS)
    )


def on_device(n_sta, n_seg, records, owners):
    own_count, seg_len = records.shape
    depth = n_sta // n_seg
    n1 = seg_len // LANES
    nk = n1 * n_seg
    blocks = own_count // BS
    slots = max(2, 2 * blocks * DESTS // n_sta)
    vmem = pl.BlockSpec(memory_space=pltpu.VMEM)
    hbm = pl.BlockSpec(memory_space=pltpu.HBM)
    constants = tables(seg_len)
    white, own, received = pl.pallas_call(
        functools.partial(gather_kernel, n_sta, n_seg),
        out_shape=(
            jax.ShapeDtypeStruct((own_count, seg_len), jnp.bfloat16),
            jax.ShapeDtypeStruct((nk + 1, own_count, LANES), jnp.bfloat16),
            jax.ShapeDtypeStruct((depth, nk + 1, own_count, LANES), jnp.bfloat16),
        ),
        in_specs=[hbm, vmem, hbm, hbm, hbm],
        out_specs=(vmem,) * 3,
        scratch_shapes=[
            pltpu.VMEM((n_seg, own_count, seg_len), jnp.bfloat16),
            *(pltpu.VMEM(table.shape, table.dtype) for table in constants),
            pltpu.VMEM((own_count, LANES), jnp.float32),
            pltpu.SemaphoreType.DMA((1 + len(constants),)),
            pltpu.SemaphoreType.DMA((n_seg - 1,)),
            pltpu.SemaphoreType.DMA((n_seg - 1,)),
            pltpu.SemaphoreType.DMA((2 * n_seg,)),
            pltpu.SemaphoreType.DMA((n_seg,)),
            pltpu.SemaphoreType.DMA((depth - 1, n_seg)),
            pltpu.SemaphoreType.DMA((depth - 1, n_seg)),
        ],
        compiler_params=pltpu.CompilerParams(
            collective_id=0, has_side_effects=True, vmem_limit_bytes=32 * 2**20
        ),
        name="whiten_and_gather",
    )(records, owners.T, *constants)
    stations = depth * own_count
    rows = depth * slots * BS
    parts = LANES // SUB
    length = (nk + LAGS // LANES + 1 + 7) // 8 * 8
    correlations = pl.pallas_call(
        functools.partial(lag_kernel, n_sta, n_seg, slots),
        out_shape=jax.ShapeDtypeStruct((rows, own_count, LAGS), jnp.bfloat16),
        in_specs=[vmem] * 2,
        out_specs=vmem,
        scratch_shapes=[
            pltpu.VMEM((nk, own_count, LANES), jnp.float32),
            pltpu.VMEM((own_count, length, LANES), jnp.float32),
            pltpu.VMEM((2, parts, length, LANES), jnp.float32),
            pltpu.VMEM((nk, own_count, LANES), jnp.float32),
            pltpu.VMEM((SUB, stations, parts * nk), jnp.float32),
            pltpu.VMEM((own_count * SUB // LANES, SUB * stations, LANES), jnp.float32),
            pltpu.VMEM((own_count, rows, LAGS), jnp.float32),
            pltpu.VMEM((rows, own_count, LAGS), jnp.float32),
        ],
        compiler_params=pltpu.CompilerParams(vmem_limit_bytes=48 * 2**20),
        name="correlate",
    )(own, received)
    return white, correlations


def solution(mesh):
    return jax.shard_map(
        functools.partial(on_device, mesh.shape["sta"], mesh.shape["seg"]),
        mesh=mesh,
        in_specs=(P("sta", "seg"), P("sta", None)),
        out_specs=(P("sta", "seg"), P("seg", "sta", None)),
        check_vma=False,
    )
```

```python
import functools
import math

import jax
import jax.numpy as jnp
from jax import lax
from jax.experimental import pallas as pl
from jax.experimental.pallas import tpu as pltpu
from jax.sharding import PartitionSpec as P

LAGS = 512
LANES = 128
BS = 2
DESTS = 4
SUB = 16

WATER = 0.5
EPSILON = 1e-06
MESH = pl.DeviceIdType.MESH


def conj(value):
    return value[0], -value[1]


def real_dft(slabs):
    n = len(slabs)
    if n == 2:
        zero = jnp.zeros_like(slabs[0])
        return [(slabs[0] + slabs[1], zero), (slabs[0] - slabs[1], zero)]
    even, odd = real_dft(slabs[::2]), real_dft(slabs[1::2])
    half = n // 2

    def at(values, k):
        k %= half
        return values[k] if k <= half // 2 else conj(values[half - k])

    result = []
    for k in range(half + 1):
        c, s = math.cos(2 * math.pi * k / n), math.sin(2 * math.pi * k / n)
        (er, ei), (pr, pi) = at(even, k), at(odd, k)
        if k == 0:
            result.append((er + pr, ei + pi))
        elif k == half:
            result.append((er - pr, ei - pi))
        elif 4 * k == n:
            result.append((er - pi, ei + pr))
        else:
            result.append((er + c * pr - s * pi, ei + s * pr + c * pi))
    return result


def real_inverse(values, n):
    if n == 2:
        return [values[0][0] + values[1][0], values[0][0] - values[1][0]]
    half = n // 2
    even, odd = [], []
    for k in range(half // 2 + 1):
        (ar, ai), (br, bi) = values[k], conj(values[half - k])
        even.append((ar + br, ai + bi))
        dr, di = ar - br, ai - bi
        c, s = math.cos(2 * math.pi * k / n), math.sin(2 * math.pi * k / n)
        if k == 0:
            odd.append((dr, di))
        elif 4 * k == n:
            odd.append((di, -dr))
        else:
            odd.append((dr * c + di * s, di * c - dr * s))
    slabs = [None] * n
    slabs[::2] = real_inverse(even, half)
    slabs[1::2] = real_inverse(odd, half)
    return slabs


def make_tables(seg_len, count):
    shape = (LANES, LANES)
    row = lax.broadcasted_iota(jnp.int32, shape, 0)
    lane = lax.broadcasted_iota(jnp.int32, shape, 1)
    angle = (row * lane % LANES).astype(jnp.float32) * (2 * math.pi / LANES)
    c, s = jnp.cos(angle).astype(jnp.bfloat16), jnp.sin(angle).astype(jnp.bfloat16)
    forward = jnp.concatenate(
        [jnp.concatenate([c, s], axis=1), jnp.concatenate([-s, c], axis=1)], axis=0
    )
    backward = jnp.concatenate(
        [jnp.concatenate([c, -s], axis=1), jnp.concatenate([s, c], axis=1)], axis=0
    )
    turn = (row * lane)[:count].astype(jnp.float32) * (2 * math.pi / seg_len)
    return jnp.cos(turn), jnp.sin(turn), forward, backward


def whiten(slabs, seg_count, own_count, cosine, sine, forward, backward):
    n1 = len(slabs)
    seg_len = n1 * LANES
    window = seg_len * seg_count
    rows = seg_count * own_count

    def over_window(value):
        total = value[:own_count]
        for g in range(1, seg_count):
            total = total + value[g * own_count : (g + 1) * own_count]
        return jnp.sum(total, axis=1, keepdims=True)

    def every_segment(value):
        return jnp.concatenate([value] * seg_count, axis=0)

    first = real_dft(slabs)
    turned = []
    for k, (re, im) in enumerate(first):
        if k:
            c, s = cosine[k : k + 1], sine[k : k + 1]
            re, im = re * c - im * s, re * s + im * c
        turned.append(jnp.concatenate([re, im], axis=1).astype(jnp.bfloat16))
    spectrum = jnp.dot(
        jnp.concatenate(turned, axis=0), forward, preferred_element_type=jnp.float32
    )
    parts, total = [], None
    for k in range(len(first)):
        re = spectrum[k * rows : (k + 1) * rows, :LANES]
        im = spectrum[k * rows : (k + 1) * rows, LANES:]
        magnitude = jnp.sqrt(re * re + im * im)
        parts.append((re, im, magnitude))
        term = magnitude if k in (0, n1 // 2) else 2.0 * magnitude
        total = term if total is None else total + term
    level = every_segment(WATER * over_window(total) / window + EPSILON)
    flat = []
    for re, im, magnitude in parts:
        inverse = 1.0 / (magnitude + level)
        flat.append(jnp.concatenate([re * inverse, im * inverse], axis=1).astype(jnp.bfloat16))
    back = jnp.dot(
        jnp.concatenate(flat, axis=0), backward, preferred_element_type=jnp.float32
    )
    turned = []
    for k in range(len(first)):
        re = back[k * rows : (k + 1) * rows, :LANES]
        im = back[k * rows : (k + 1) * rows, LANES:]
        if k:
            c, s = cosine[k : k + 1], sine[k : k + 1]
            re, im = re * c + im * s, im * c - re * s
        turned.append((re, im))
    trace = [slab * (1.0 / seg_len) for slab in real_inverse(turned, n1)]
    squares = trace[0] * trace[0]
    for slab in trace[1:]:
        squares = squares + slab * slab
    scale = every_segment(lax.rsqrt(over_window(squares) / window + EPSILON))
    return [slab * scale for slab in trace]


def gather_kernel(
    n_sta,
    n_seg,
    records,
    owners,
    own,
    received,
    held,
    names,
    seg_send,
    seg_recv,
    z_send,
    z_recv,
    y_send,
    y_recv,
):
    depth = n_sta // n_seg
    planes = n_seg
    own_count, seg_len = records.shape
    n1 = seg_len // LANES
    g, s = lax.axis_index("seg"), lax.axis_index("sta")
    z, y = s // depth, s % depth

    names[...] = jnp.zeros_like(names)
    names[: owners.shape[0], : owners.shape[1]] = owners[...].astype(jnp.float32)
    barrier = pltpu.get_barrier_semaphore()
    for d in range(1, n_seg):
        pl.semaphore_signal(barrier, inc=1, device_id={"seg": (g + d) % n_seg}, device_id_type=MESH)
    for d in range(1, depth):
        pl.semaphore_signal(
            barrier, inc=1, device_id={"sta": z * depth + (y + d) % depth}, device_id_type=MESH
        )

    @pl.when(z > 0)
    def _():
        pl.semaphore_signal(barrier, inc=1, device_id={"sta": s - depth}, device_id_type=MESH)

    @pl.when(z < planes - 1)
    def _():
        pl.semaphore_signal(barrier, inc=1, device_id={"sta": s + depth}, device_id_type=MESH)

    below, above = (z + planes - 1) // planes, (2 * planes - 2 - z) // planes
    pl.semaphore_wait(barrier, n_seg - 1 + depth - 1 + below + above)

    copies = []
    for d in range(1, n_seg):
        copy = pltpu.make_async_remote_copy(
            src_ref=records,
            dst_ref=held.at[g],
            send_sem=seg_send.at[d - 1],
            recv_sem=seg_recv.at[d - 1],
            device_id={"seg": (g + d) % n_seg},
            device_id_type=MESH,
        )
        copy.start()
        copies.append(copy)
    held[g] = records[...]
    made = make_tables(seg_len, (n1 // 2 + 8) // 8 * 8)
    for copy in copies:
        copy.wait()

    slabs = []
    for t in range(n1):
        slabs.append(
            jnp.concatenate(
                [held[j, :, t * LANES : (t + 1) * LANES].astype(jnp.float32) for j in range(n_seg)],
                axis=0,
            )
        )
    result = whiten(slabs, n_seg, own_count, *made)
    for t in range(n1):
        rounded = result[t].astype(jnp.bfloat16)
        for j in range(n_seg):
            own[j * n1 + t] = rounded[j * own_count : (j + 1) * own_count]
    own[n_seg * n1] = names[...].astype(jnp.bfloat16)

    @pl.when(z == g)
    def _():
        received[y] = own[...]

    up = jnp.logical_and(z >= g, z < planes - 1)
    down = jnp.logical_and(z <= g, z > 0)

    def along_z(j, target):
        size = n1 + (1 if j == n_seg - 1 else 0)
        part = received.at[y, pl.ds(j * n1, size)]
        return pltpu.make_async_remote_copy(
            src_ref=part,
            dst_ref=part,
            send_sem=z_send.at[j],
            recv_sem=z_recv.at[j],
            device_id={"sta": target},
            device_id_type=MESH,
        )

    def along_z_up(j):
        return along_z(j, s + depth)

    def along_z_down(j):
        size = n1 + (1 if j == n_seg - 1 else 0)
        part = received.at[y, pl.ds(j * n1, size)]
        return pltpu.make_async_remote_copy(
            src_ref=part,
            dst_ref=part,
            send_sem=z_send.at[n_seg + j],
            recv_sem=z_recv.at[j],
            device_id={"sta": s - depth},
            device_id_type=MESH,
        )

    def along_y(j, d):
        size = n1 + (1 if j == n_seg - 1 else 0)
        part = received.at[y, pl.ds(j * n1, size)]
        return pltpu.make_async_remote_copy(
            src_ref=part,
            dst_ref=part,
            send_sem=y_send.at[d - 1, j],
            recv_sem=y_recv.at[d - 1, j],
            device_id={"sta": z * depth + (y + d) % depth},
            device_id_type=MESH,
        )

    for j in range(n_seg):

        @pl.when(z != g)
        def _():
            along_z_up(j).wait_recv()

        @pl.when(up)
        def _():
            along_z_up(j).start()

        @pl.when(down)
        def _():
            along_z_down(j).start()

        for d in range(1, depth):
            along_y(j, d).start()
    for j in range(n_seg):
        for d in range(1, depth):
            along_y(j, d).wait()

        @pl.when(up)
        def _():
            along_z_up(j).wait_send()

        @pl.when(down)
        def _():
            along_z_down(j).wait_send()


def lag_kernel(n_sta, n_seg, slots, own, received, white, out, flat, series, turned, shifted, rec, left, tails, grams, sums, order):
    depth = n_sta // n_seg
    nk, own_count = own.shape[0] - 1, own.shape[1]
    stations = depth * own_count
    parts = LANES // SUB
    tiles = LAGS // LANES
    edge = LAGS // 2 // LANES
    per_tile = LANES // SUB
    me = lax.axis_index("sta").astype(jnp.float32)
    length = series.shape[1]

    g = lax.axis_index("seg")
    n1 = nk // n_seg
    for t in range(n1):
        white[:, t * LANES : (t + 1) * LANES] = own[g * n1 + t]

    flat[...] = own[:nk].astype(jnp.float32)
    series[...] = jnp.zeros_like(series)
    for a in range(own_count):
        series[a, edge : edge + nk] = flat[:, a, :]

    for y in range(depth):
        rec[...] = received[y, :nk].astype(jnp.float32)
        for b in range(own_count):
            across = rec[:, b, :].T
            left[:, y * own_count + b, :] = jnp.concatenate(
                [across[c * SUB : (c + 1) * SUB] for c in range(parts)], axis=1
            )
    lhs = left[...].reshape(SUB * stations, parts * nk).astype(jnp.bfloat16)

    lane = lax.broadcasted_iota(jnp.int32, (nk, LANES), 1)
    for first in range(0, own_count, per_tile):
        pieces = []
        for c in range(parts):
            piece = jnp.zeros((nk, LANES), jnp.float32)
            for q in range(per_tile):
                shift = (SUB * q - SUB * c - 1) % LANES
                moved = series[first + q, tiles : tiles + nk]
                moved = pltpu.roll(moved, shift, 1) if shift else moved
                piece = jnp.where(lane // SUB == q, moved, piece)
            pieces.append(piece)
        ends_of = jnp.dot(
            lhs,
            jnp.concatenate(pieces, axis=0).astype(jnp.bfloat16),
            preferred_element_type=jnp.float32,
        )
        place = lax.broadcasted_iota(jnp.int32, (stations, LANES), 1)
        added = jnp.zeros((stations, LANES), jnp.float32)
        for i in range(1, SUB):
            part = jnp.where(place % SUB < i, ends_of[i * stations : (i + 1) * stations], 0.0)
            added += pltpu.roll(part, SUB - i, 1)
        tails[first // per_tile] = added

    shape = (stations, stations)
    row = lax.broadcasted_iota(jnp.int32, shape, 0)
    station = lax.broadcasted_iota(jnp.int32, shape, 1)
    source, block = station // own_count, station % own_count // BS
    wide = (LANES, stations)
    number = lax.broadcasted_iota(jnp.int32, wide, 0)
    wide_station = lax.broadcasted_iota(jnp.int32, wide, 1)
    wide_block = wide_station % own_count // BS
    entry = lax.broadcasted_iota(jnp.int32, (own_count, LANES), 0)
    wanted = jnp.zeros(shape, jnp.float32)
    rank = jnp.zeros(shape, jnp.float32)
    for y in range(depth):
        names = received[y, nk].astype(jnp.float32)
        named = jnp.max(
            jnp.where(jnp.logical_and(entry < DESTS, names == me), 1.0, 0.0), axis=0, keepdims=True
        )
        named = jnp.broadcast_to(named, (stations, LANES)).astype(jnp.bfloat16)
        here = wide_station // own_count == y
        same = jnp.where(jnp.logical_and(here, number == wide_block), 1.0, 0.0)
        before = jnp.where(jnp.logical_and(here, number < wide_block), 1.0, 0.0)
        wanted += jnp.dot(named, same.astype(jnp.bfloat16), preferred_element_type=jnp.float32)
        rank += jnp.dot(named, before.astype(jnp.bfloat16), preferred_element_type=jnp.float32)
    slot = (row // BS % slots).astype(jnp.float32)
    hit = jnp.logical_and(row // (BS * slots) == source, row % BS == station % BS)
    hit = jnp.logical_and(hit, slot == rank)
    select = jnp.where(hit, wanted, 0.0).astype(jnp.bfloat16)
    rows = out.shape[0]
    window = nk * LANES
    scale = 1.0 / math.sqrt(window)
    last = lax.broadcasted_iota(jnp.int32, (stations, LANES), 1) >= LANES - SUB
    across_lanes = lax.broadcasted_iota(jnp.int32, (8, LAGS), 1)
    whole_lane = lax.broadcasted_iota(jnp.int32, (length - 8, LANES), 1)

    def one_station(a, half):
        whole = series[a]
        pieces = []
        for c in range(parts):
            shift = LANES - SUB * c - 1
            moved = pltpu.roll(whole, shift, 1)
            turned[half, c] = moved
            shifted[half, c] = jnp.where(
                whole_lane < shift, moved[: length - 8], turned[half, c, 1 : length - 7]
            )
            pieces.append(
                jnp.concatenate(
                    [shifted[half, c, v : v + nk] for v in range(tiles)], axis=1
                ).astype(jnp.bfloat16)
            )
        grams[half] = jnp.dot(
            lhs, jnp.concatenate(pieces, axis=0), preferred_element_type=jnp.float32
        )
        totals = []
        for r in range(0, stations, 8):
            total = jnp.zeros((8, LAGS), jnp.float32)
            for i in reversed(range(SUB)):
                term = grams[half, i * stations + r : i * stations + r + 8]
                if i < SUB - 1:
                    total = pltpu.roll(total, LAGS - 1, 1)
                total = total + (jnp.where(across_lanes < i, 0.0, term) if i else term)
            totals.append(total)
        total = jnp.concatenate(totals, axis=0)
        move = (LANES - SUB - SUB * (a % per_tile)) % LANES
        tail = pltpu.roll(tails[a // per_tile], move, 1)
        edge_tile = total[:, LAGS - LANES :] + jnp.where(last, tail, 0.0)
        total = jnp.concatenate([total[:, : LAGS - LANES], edge_tile], axis=1)
        sums[a] = jnp.dot(
            select, (total * scale).astype(jnp.bfloat16), preferred_element_type=jnp.float32
        )[:rows]

    def pair(step, carry):
        one_station(2 * step, 0)
        one_station(2 * step + 1, 1)
        return carry

    lax.fori_loop(0, own_count // 2, pair, 0)
    for a in range(own_count):
        order[:, a, :] = sums[a]
    square = (LAGS, LAGS)
    ends = lax.broadcasted_iota(jnp.int32, square, 0) + lax.broadcasted_iota(jnp.int32, square, 1)
    flip = jnp.where(ends == LAGS - 1, 1.0, 0.0).astype(jnp.bfloat16)
    out[...] = (
        jnp.dot(
            order[...].reshape(rows * own_count, LAGS).astype(jnp.bfloat16),
            flip,
            preferred_element_type=jnp.float32,
        )
        .astype(jnp.bfloat16)
        .reshape(rows, own_count, LAGS)
    )


def on_device(n_sta, n_seg, records, owners):
    own_count, seg_len = records.shape
    depth = n_sta // n_seg
    n1 = seg_len // LANES
    nk = n1 * n_seg
    blocks = own_count // BS
    slots = max(2, 2 * blocks * DESTS // n_sta)
    vmem = pl.BlockSpec(memory_space=pltpu.VMEM)
    own, received = pl.pallas_call(
        functools.partial(gather_kernel, n_sta, n_seg),
        out_shape=(
            jax.ShapeDtypeStruct((nk + 1, own_count, LANES), jnp.bfloat16),
            jax.ShapeDtypeStruct((depth, nk + 1, own_count, LANES), jnp.bfloat16),
        ),
        in_specs=[vmem] * 2,
        out_specs=(vmem,) * 2,
        scratch_shapes=[
            pltpu.VMEM((n_seg, own_count, seg_len), jnp.bfloat16),
            pltpu.VMEM((own_count, LANES), jnp.float32),
            pltpu.SemaphoreType.DMA((n_seg - 1,)),
            pltpu.SemaphoreType.DMA((n_seg - 1,)),
            pltpu.SemaphoreType.DMA((2 * n_seg,)),
            pltpu.SemaphoreType.DMA((n_seg,)),
            pltpu.SemaphoreType.DMA((depth - 1, n_seg)),
            pltpu.SemaphoreType.DMA((depth - 1, n_seg)),
        ],
        compiler_params=pltpu.CompilerParams(
            collective_id=0, has_side_effects=True, vmem_limit_bytes=32 * 2**20
        ),
        name="whiten_and_gather",
    )(records, owners.T)
    stations = depth * own_count
    rows = depth * slots * BS
    parts = LANES // SUB
    length = (nk + LAGS // LANES + 7) // 8 * 8 + 8
    white, correlations = pl.pallas_call(
        functools.partial(lag_kernel, n_sta, n_seg, slots),
        out_shape=(
            jax.ShapeDtypeStruct((own_count, seg_len), jnp.bfloat16),
            jax.ShapeDtypeStruct((rows, own_count, LAGS), jnp.bfloat16),
        ),
        in_specs=[vmem] * 2,
        out_specs=(vmem,) * 2,
        scratch_shapes=[
            pltpu.VMEM((nk, own_count, LANES), jnp.float32),
            pltpu.VMEM((own_count, length, LANES), jnp.float32),
            pltpu.VMEM((2, parts, length, LANES), jnp.float32),
            pltpu.VMEM((2, parts, length - 8, LANES), jnp.float32),
            pltpu.VMEM((nk, own_count, LANES), jnp.float32),
            pltpu.VMEM((SUB, stations, parts * nk), jnp.float32),
            pltpu.VMEM((own_count * SUB // LANES, stations, LANES), jnp.float32),
            pltpu.VMEM((2, SUB * stations, LAGS), jnp.float32),
            pltpu.VMEM((own_count, rows, LAGS), jnp.float32),
            pltpu.VMEM((rows, own_count, LAGS), jnp.float32),
        ],
        compiler_params=pltpu.CompilerParams(vmem_limit_bytes=48 * 2**20),
        name="correlate",
    )(own, received)
    return white, correlations


def solution(mesh):
    return jax.shard_map(
        functools.partial(on_device, mesh.shape["sta"], mesh.shape["seg"]),
        mesh=mesh,
        in_specs=(P("sta", "seg"), P("sta", None)),
        out_specs=(P("sta", "seg"), P("seg", "sta", None)),
        check_vma=False,
    )
```

```python
import functools
import math

import jax
import jax.numpy as jnp
from jax import lax
from jax.experimental import pallas as pl
from jax.experimental.pallas import tpu as pltpu
from jax.sharding import PartitionSpec as P

LAGS = 512
LANES = 128
BS = 2
DESTS = 4
SUB = 16

WATER = 0.5
EPSILON = 1e-06
MESH = pl.DeviceIdType.MESH


def conj(value):
    return value[0], -value[1]


def real_dft(slabs):
    n = len(slabs)
    if n == 2:
        zero = jnp.zeros_like(slabs[0])
        return [(slabs[0] + slabs[1], zero), (slabs[0] - slabs[1], zero)]
    even, odd = real_dft(slabs[::2]), real_dft(slabs[1::2])
    half = n // 2

    def at(values, k):
        k %= half
        return values[k] if k <= half // 2 else conj(values[half - k])

    result = []
    for k in range(half + 1):
        c, s = math.cos(2 * math.pi * k / n), math.sin(2 * math.pi * k / n)
        (er, ei), (pr, pi) = at(even, k), at(odd, k)
        if k == 0:
            result.append((er + pr, ei + pi))
        elif k == half:
            result.append((er - pr, ei - pi))
        elif 4 * k == n:
            result.append((er - pi, ei + pr))
        else:
            result.append((er + c * pr - s * pi, ei + s * pr + c * pi))
    return result


def real_inverse(values, n):
    if n == 2:
        return [values[0][0] + values[1][0], values[0][0] - values[1][0]]
    half = n // 2
    even, odd = [], []
    for k in range(half // 2 + 1):
        (ar, ai), (br, bi) = values[k], conj(values[half - k])
        even.append((ar + br, ai + bi))
        dr, di = ar - br, ai - bi
        c, s = math.cos(2 * math.pi * k / n), math.sin(2 * math.pi * k / n)
        if k == 0:
            odd.append((dr, di))
        elif 4 * k == n:
            odd.append((di, -dr))
        else:
            odd.append((dr * c + di * s, di * c - dr * s))
    slabs = [None] * n
    slabs[::2] = real_inverse(even, half)
    slabs[1::2] = real_inverse(odd, half)
    return slabs


def make_tables(seg_len, count):
    shape = (LANES, LANES)
    row = lax.broadcasted_iota(jnp.int32, shape, 0)
    lane = lax.broadcasted_iota(jnp.int32, shape, 1)
    angle = (row * lane % LANES).astype(jnp.float32) * (2 * math.pi / LANES)
    c, s = jnp.cos(angle).astype(jnp.bfloat16), jnp.sin(angle).astype(jnp.bfloat16)
    forward = jnp.concatenate(
        [jnp.concatenate([c, s], axis=1), jnp.concatenate([-s, c], axis=1)], axis=0
    )
    backward = jnp.concatenate(
        [jnp.concatenate([c, -s], axis=1), jnp.concatenate([s, c], axis=1)], axis=0
    )
    turn = (row * lane)[:count].astype(jnp.float32) * (2 * math.pi / seg_len)
    return jnp.cos(turn), jnp.sin(turn), forward, backward


def whiten(slabs, seg_count, own_count, cosine, sine, forward, backward):
    n1 = len(slabs)
    seg_len = n1 * LANES
    window = seg_len * seg_count
    rows = seg_count * own_count

    def over_window(value):
        total = value[:own_count]
        for g in range(1, seg_count):
            total = total + value[g * own_count : (g + 1) * own_count]
        return jnp.sum(total, axis=1, keepdims=True)

    def every_segment(value):
        return jnp.concatenate([value] * seg_count, axis=0)

    first = real_dft(slabs)
    turned = []
    for k, (re, im) in enumerate(first):
        if k:
            c, s = cosine[k : k + 1], sine[k : k + 1]
            re, im = re * c - im * s, re * s + im * c
        turned.append(jnp.concatenate([re, im], axis=1).astype(jnp.bfloat16))
    spectrum = jnp.dot(
        jnp.concatenate(turned, axis=0), forward, preferred_element_type=jnp.float32
    )
    parts, total = [], None
    for k in range(len(first)):
        re = spectrum[k * rows : (k + 1) * rows, :LANES]
        im = spectrum[k * rows : (k + 1) * rows, LANES:]
        magnitude = jnp.sqrt(re * re + im * im)
        parts.append((re, im, magnitude))
        term = magnitude if k in (0, n1 // 2) else 2.0 * magnitude
        total = term if total is None else total + term
    level = every_segment(WATER * over_window(total) / window + EPSILON)
    flat = []
    for re, im, magnitude in parts:
        inverse = 1.0 / (magnitude + level)
        flat.append(jnp.concatenate([re * inverse, im * inverse], axis=1).astype(jnp.bfloat16))
    back = jnp.dot(
        jnp.concatenate(flat, axis=0), backward, preferred_element_type=jnp.float32
    )
    turned = []
    for k in range(len(first)):
        re = back[k * rows : (k + 1) * rows, :LANES]
        im = back[k * rows : (k + 1) * rows, LANES:]
        if k:
            c, s = cosine[k : k + 1], sine[k : k + 1]
            re, im = re * c + im * s, im * c - re * s
        turned.append((re, im))
    trace = [slab * (1.0 / seg_len) for slab in real_inverse(turned, n1)]
    squares = trace[0] * trace[0]
    for slab in trace[1:]:
        squares = squares + slab * slab
    scale = every_segment(lax.rsqrt(over_window(squares) / window + EPSILON))
    return [slab * scale for slab in trace]


def gather_kernel(
    n_sta,
    n_seg,
    records,
    owners,
    own,
    series,
    received,
    held,
    names,
    flat,
    seg_send,
    seg_recv,
    z_send,
    z_recv,
    y_send,
    y_recv,
):
    depth = n_sta // n_seg
    planes = n_seg
    own_count, seg_len = records.shape
    n1 = seg_len // LANES
    g, s = lax.axis_index("seg"), lax.axis_index("sta")
    z, y = s // depth, s % depth

    names[...] = jnp.zeros_like(names)
    names[: owners.shape[0], : owners.shape[1]] = owners[...].astype(jnp.float32)
    barrier = pltpu.get_barrier_semaphore()
    for d in range(1, n_seg):
        pl.semaphore_signal(barrier, inc=1, device_id={"seg": (g + d) % n_seg}, device_id_type=MESH)
    for d in range(1, depth):
        pl.semaphore_signal(
            barrier, inc=1, device_id={"sta": z * depth + (y + d) % depth}, device_id_type=MESH
        )

    @pl.when(z > 0)
    def _():
        pl.semaphore_signal(barrier, inc=1, device_id={"sta": s - depth}, device_id_type=MESH)

    @pl.when(z < planes - 1)
    def _():
        pl.semaphore_signal(barrier, inc=1, device_id={"sta": s + depth}, device_id_type=MESH)

    below, above = (z + planes - 1) // planes, (2 * planes - 2 - z) // planes
    pl.semaphore_wait(barrier, n_seg - 1 + depth - 1 + below + above)

    copies = []
    for d in range(1, n_seg):
        copy = pltpu.make_async_remote_copy(
            src_ref=records,
            dst_ref=held.at[g],
            send_sem=seg_send.at[d - 1],
            recv_sem=seg_recv.at[d - 1],
            device_id={"seg": (g + d) % n_seg},
            device_id_type=MESH,
        )
        copy.start()
        copies.append(copy)
    held[g] = records[...]
    made = make_tables(seg_len, (n1 // 2 + 8) // 8 * 8)
    for copy in copies:
        copy.wait()

    slabs = []
    for t in range(n1):
        slabs.append(
            jnp.concatenate(
                [held[j, :, t * LANES : (t + 1) * LANES].astype(jnp.float32) for j in range(n_seg)],
                axis=0,
            )
        )
    result = whiten(slabs, n_seg, own_count, *made)
    for t in range(n1):
        rounded = result[t].astype(jnp.bfloat16)
        for j in range(n_seg):
            own[j * n1 + t] = rounded[j * own_count : (j + 1) * own_count]
            flat[j * n1 + t] = rounded[j * own_count : (j + 1) * own_count].astype(jnp.float32)
    own[n_seg * n1] = names[...].astype(jnp.bfloat16)

    @pl.when(z == g)
    def _():
        received[y] = own[...]

    up = jnp.logical_and(z >= g, z < planes - 1)
    down = jnp.logical_and(z <= g, z > 0)

    def along_z(j, target):
        size = n1 + (1 if j == n_seg - 1 else 0)
        part = received.at[y, pl.ds(j * n1, size)]
        return pltpu.make_async_remote_copy(
            src_ref=part,
            dst_ref=part,
            send_sem=z_send.at[j],
            recv_sem=z_recv.at[j],
            device_id={"sta": target},
            device_id_type=MESH,
        )

    def along_z_up(j):
        return along_z(j, s + depth)

    def along_z_down(j):
        size = n1 + (1 if j == n_seg - 1 else 0)
        part = received.at[y, pl.ds(j * n1, size)]
        return pltpu.make_async_remote_copy(
            src_ref=part,
            dst_ref=part,
            send_sem=z_send.at[n_seg + j],
            recv_sem=z_recv.at[j],
            device_id={"sta": s - depth},
            device_id_type=MESH,
        )

    def along_y(j, d):
        size = n1 + (1 if j == n_seg - 1 else 0)
        part = received.at[y, pl.ds(j * n1, size)]
        return pltpu.make_async_remote_copy(
            src_ref=part,
            dst_ref=part,
            send_sem=y_send.at[d - 1, j],
            recv_sem=y_recv.at[d - 1, j],
            device_id={"sta": z * depth + (y + d) % depth},
            device_id_type=MESH,
        )

    def send(j):
        @pl.when(up)
        def _():
            along_z_up(j).start()

        @pl.when(down)
        def _():
            along_z_down(j).start()

        for d in range(1, depth):
            along_y(j, d).start()

    @pl.when(z == g)
    def _():
        for j in range(n_seg):
            send(j)

    edge = LAGS // 2 // LANES
    series[...] = jnp.zeros_like(series)
    for a in range(own_count):
        series[a, edge : edge + n_seg * n1] = flat[:, a, :]

    @pl.when(z != g)
    def _():
        for j in range(n_seg):
            along_z_up(j).wait_recv()
            send(j)

    for j in range(n_seg):
        for d in range(1, depth):
            along_y(j, d).wait()

        @pl.when(up)
        def _():
            along_z_up(j).wait_send()

        @pl.when(down)
        def _():
            along_z_down(j).wait_send()


def lag_kernel(n_sta, n_seg, slots, own, series, received, white, out, turned, shifted, rec, left, tails, grams, sums, order):
    depth = n_sta // n_seg
    nk, own_count = own.shape[0] - 1, own.shape[1]
    stations = depth * own_count
    parts = LANES // SUB
    tiles = LAGS // LANES
    per_tile = LANES // SUB
    me = lax.axis_index("sta").astype(jnp.float32)
    length = series.shape[1]

    g = lax.axis_index("seg")
    n1 = nk // n_seg
    for t in range(n1):
        white[:, t * LANES : (t + 1) * LANES] = own[g * n1 + t]

    for y in range(depth):
        rec[...] = received[y, :nk].astype(jnp.float32)
        for b in range(own_count):
            across = rec[:, b, :].T
            left[:, y * own_count + b, :] = jnp.concatenate(
                [across[c * SUB : (c + 1) * SUB] for c in range(parts)], axis=1
            )
    lhs = left[...].reshape(SUB * stations, parts * nk).astype(jnp.bfloat16)

    lane = lax.broadcasted_iota(jnp.int32, (nk, LANES), 1)
    for first in range(0, own_count, per_tile):
        pieces = []
        for c in range(parts):
            piece = jnp.zeros((nk, LANES), jnp.float32)
            for q in range(per_tile):
                shift = (SUB * q - SUB * c - 1) % LANES
                moved = series[first + q, tiles : tiles + nk]
                moved = pltpu.roll(moved, shift, 1) if shift else moved
                piece = jnp.where(lane // SUB == q, moved, piece)
            pieces.append(piece)
        ends_of = jnp.dot(
            lhs,
            jnp.concatenate(pieces, axis=0).astype(jnp.bfloat16),
            preferred_element_type=jnp.float32,
        )
        place = lax.broadcasted_iota(jnp.int32, (stations, LANES), 1)
        added = jnp.zeros((stations, LANES), jnp.float32)
        for i in range(1, SUB):
            part = jnp.where(place % SUB < i, ends_of[i * stations : (i + 1) * stations], 0.0)
            added += pltpu.roll(part, SUB - i, 1)
        tails[first // per_tile] = added

    shape = (stations, stations)
    row = lax.broadcasted_iota(jnp.int32, shape, 0)
    station = lax.broadcasted_iota(jnp.int32, shape, 1)
    source, block = station // own_count, station % own_count // BS
    wide = (LANES, stations)
    number = lax.broadcasted_iota(jnp.int32, wide, 0)
    wide_station = lax.broadcasted_iota(jnp.int32, wide, 1)
    wide_block = wide_station % own_count // BS
    entry = lax.broadcasted_iota(jnp.int32, (own_count, LANES), 0)
    wanted = jnp.zeros(shape, jnp.float32)
    rank = jnp.zeros(shape, jnp.float32)
    for y in range(depth):
        names = received[y, nk].astype(jnp.float32)
        named = jnp.max(
            jnp.where(jnp.logical_and(entry < DESTS, names == me), 1.0, 0.0), axis=0, keepdims=True
        )
        named = jnp.broadcast_to(named, (stations, LANES)).astype(jnp.bfloat16)
        here = wide_station // own_count == y
        same = jnp.where(jnp.logical_and(here, number == wide_block), 1.0, 0.0)
        before = jnp.where(jnp.logical_and(here, number < wide_block), 1.0, 0.0)
        wanted += jnp.dot(named, same.astype(jnp.bfloat16), preferred_element_type=jnp.float32)
        rank += jnp.dot(named, before.astype(jnp.bfloat16), preferred_element_type=jnp.float32)
    slot = (row // BS % slots).astype(jnp.float32)
    hit = jnp.logical_and(row // (BS * slots) == source, row % BS == station % BS)
    hit = jnp.logical_and(hit, slot == rank)
    select = jnp.where(hit, wanted, 0.0).astype(jnp.bfloat16)
    rows = out.shape[0]
    window = nk * LANES
    scale = 1.0 / math.sqrt(window)
    lag_lane = lax.broadcasted_iota(jnp.int32, (stations, LANES), 1)
    last = lag_lane >= LANES - SUB
    whole_lane = lax.broadcasted_iota(jnp.int32, (length - 8, LANES), 1)

    def one_station(a, half):
        whole = series[a]
        pieces = []
        for c in range(parts):
            shift = LANES - SUB * c - 1
            moved = pltpu.roll(whole, shift, 1)
            turned[half, c] = moved
            shifted[half, c] = jnp.where(
                whole_lane < shift, moved[: length - 8], turned[half, c, 1 : length - 7]
            )
            pieces.append(
                jnp.concatenate(
                    [shifted[half, c, v : v + nk] for v in range(tiles)], axis=1
                ).astype(jnp.bfloat16)
            )
        grams[half] = jnp.dot(
            lhs, jnp.concatenate(pieces, axis=0), preferred_element_type=jnp.float32
        )

        def diagonal(first, count):
            if count == 1:
                term = grams[half, first * stations : (first + 1) * stations]
                head = jnp.where(lag_lane < first, 0.0, term[:, :LANES])
                return jnp.concatenate([head, term[:, LANES:]], axis=1) if first else term
            count //= 2
            later = pltpu.roll(diagonal(first + count, count), LAGS - count, 1)
            return diagonal(first, count) + later

        total = diagonal(0, SUB)
        move = (LANES - SUB - SUB * (a % per_tile)) % LANES
        tail = pltpu.roll(tails[a // per_tile], move, 1)
        edge_tile = total[:, LAGS - LANES :] + jnp.where(last, tail, 0.0)
        total = jnp.concatenate([total[:, : LAGS - LANES], edge_tile], axis=1)
        sums[a] = jnp.dot(
            select, (total * scale).astype(jnp.bfloat16), preferred_element_type=jnp.float32
        )[:rows]

    def pair(step, carry):
        one_station(2 * step, 0)
        one_station(2 * step + 1, 1)
        return carry

    lax.fori_loop(0, own_count // 2, pair, 0)
    for a in range(own_count):
        order[:, a, :] = sums[a]
    square = (LAGS, LAGS)
    ends = lax.broadcasted_iota(jnp.int32, square, 0) + lax.broadcasted_iota(jnp.int32, square, 1)
    flip = jnp.where(ends == LAGS - 1, 1.0, 0.0).astype(jnp.bfloat16)
    out[...] = (
        jnp.dot(
            order[...].reshape(rows * own_count, LAGS).astype(jnp.bfloat16),
            flip,
            preferred_element_type=jnp.float32,
        )
        .astype(jnp.bfloat16)
        .reshape(rows, own_count, LAGS)
    )


def on_device(n_sta, n_seg, records, owners):
    own_count, seg_len = records.shape
    depth = n_sta // n_seg
    n1 = seg_len // LANES
    nk = n1 * n_seg
    length = (nk + LAGS // LANES + 7) // 8 * 8 + 8
    blocks = own_count // BS
    slots = max(2, 2 * blocks * DESTS // n_sta)
    vmem = pl.BlockSpec(memory_space=pltpu.VMEM)
    own, series, received = pl.pallas_call(
        functools.partial(gather_kernel, n_sta, n_seg),
        out_shape=(
            jax.ShapeDtypeStruct((nk + 1, own_count, LANES), jnp.bfloat16),
            jax.ShapeDtypeStruct((own_count, length, LANES), jnp.float32),
            jax.ShapeDtypeStruct((depth, nk + 1, own_count, LANES), jnp.bfloat16),
        ),
        in_specs=[vmem] * 2,
        out_specs=(vmem,) * 3,
        scratch_shapes=[
            pltpu.VMEM((n_seg, own_count, seg_len), jnp.bfloat16),
            pltpu.VMEM((own_count, LANES), jnp.float32),
            pltpu.VMEM((nk, own_count, LANES), jnp.float32),
            pltpu.SemaphoreType.DMA((n_seg - 1,)),
            pltpu.SemaphoreType.DMA((n_seg - 1,)),
            pltpu.SemaphoreType.DMA((2 * n_seg,)),
            pltpu.SemaphoreType.DMA((n_seg,)),
            pltpu.SemaphoreType.DMA((depth - 1, n_seg)),
            pltpu.SemaphoreType.DMA((depth - 1, n_seg)),
        ],
        compiler_params=pltpu.CompilerParams(
            collective_id=0, has_side_effects=True, vmem_limit_bytes=32 * 2**20
        ),
        name="whiten_and_gather",
    )(records, owners.T)
    stations = depth * own_count
    rows = depth * slots * BS
    parts = LANES // SUB
    white, correlations = pl.pallas_call(
        functools.partial(lag_kernel, n_sta, n_seg, slots),
        out_shape=(
            jax.ShapeDtypeStruct((own_count, seg_len), jnp.bfloat16),
            jax.ShapeDtypeStruct((rows, own_count, LAGS), jnp.bfloat16),
        ),
        in_specs=[vmem] * 3,
        out_specs=(vmem,) * 2,
        scratch_shapes=[
            pltpu.VMEM((2, parts, length, LANES), jnp.float32),
            pltpu.VMEM((2, parts, length - 8, LANES), jnp.float32),
            pltpu.VMEM((nk, own_count, LANES), jnp.float32),
            pltpu.VMEM((SUB, stations, parts * nk), jnp.float32),
            pltpu.VMEM((own_count * SUB // LANES, stations, LANES), jnp.float32),
            pltpu.VMEM((2, SUB * stations, LAGS), jnp.float32),
            pltpu.VMEM((own_count, rows, LAGS), jnp.float32),
            pltpu.VMEM((rows, own_count, LAGS), jnp.float32),
        ],
        compiler_params=pltpu.CompilerParams(vmem_limit_bytes=48 * 2**20),
        name="correlate",
    )(own, series, received)
    return white, correlations


def solution(mesh):
    return jax.shard_map(
        functools.partial(on_device, mesh.shape["sta"], mesh.shape["seg"]),
        mesh=mesh,
        in_specs=(P("sta", "seg"), P("sta", None)),
        out_specs=(P("sta", "seg"), P("seg", "sta", None)),
        check_vma=False,
    )
```

```python
import functools
import math

import jax
import jax.numpy as jnp
from jax import lax
from jax.experimental import pallas as pl
from jax.experimental.pallas import tpu as pltpu
from jax.sharding import PartitionSpec as P

LAGS = 512
LANES = 128
BS = 2
DESTS = 4
SUB = 16

WATER = 0.5
EPSILON = 1e-06
MESH = pl.DeviceIdType.MESH


def conj(value):
    return value[0], -value[1]


def real_dft(slabs):
    n = len(slabs)
    if n == 2:
        zero = jnp.zeros_like(slabs[0])
        return [(slabs[0] + slabs[1], zero), (slabs[0] - slabs[1], zero)]
    even, odd = real_dft(slabs[::2]), real_dft(slabs[1::2])
    half = n // 2

    def at(values, k):
        k %= half
        return values[k] if k <= half // 2 else conj(values[half - k])

    result = []
    for k in range(half + 1):
        c, s = math.cos(2 * math.pi * k / n), math.sin(2 * math.pi * k / n)
        (er, ei), (pr, pi) = at(even, k), at(odd, k)
        if k == 0:
            result.append((er + pr, ei + pi))
        elif k == half:
            result.append((er - pr, ei - pi))
        elif 4 * k == n:
            result.append((er - pi, ei + pr))
        else:
            result.append((er + c * pr - s * pi, ei + s * pr + c * pi))
    return result


def real_inverse(values, n):
    if n == 2:
        return [values[0][0] + values[1][0], values[0][0] - values[1][0]]
    half = n // 2
    even, odd = [], []
    for k in range(half // 2 + 1):
        (ar, ai), (br, bi) = values[k], conj(values[half - k])
        even.append((ar + br, ai + bi))
        dr, di = ar - br, ai - bi
        c, s = math.cos(2 * math.pi * k / n), math.sin(2 * math.pi * k / n)
        if k == 0:
            odd.append((dr, di))
        elif 4 * k == n:
            odd.append((di, -dr))
        else:
            odd.append((dr * c + di * s, di * c - dr * s))
    slabs = [None] * n
    slabs[::2] = real_inverse(even, half)
    slabs[1::2] = real_inverse(odd, half)
    return slabs


def make_tables(seg_len, count):
    shape = (LANES, LANES)
    row = lax.broadcasted_iota(jnp.int32, shape, 0)
    lane = lax.broadcasted_iota(jnp.int32, shape, 1)
    angle = (row * lane % LANES).astype(jnp.float32) * (2 * math.pi / LANES)
    c, s = jnp.cos(angle).astype(jnp.bfloat16), jnp.sin(angle).astype(jnp.bfloat16)
    forward = jnp.concatenate(
        [jnp.concatenate([c, s], axis=1), jnp.concatenate([-s, c], axis=1)], axis=0
    )
    backward = jnp.concatenate(
        [jnp.concatenate([c, -s], axis=1), jnp.concatenate([s, c], axis=1)], axis=0
    )
    turn = (row * lane)[:count].astype(jnp.float32) * (2 * math.pi / seg_len)
    return jnp.cos(turn), jnp.sin(turn), forward, backward


def whiten(slabs, seg_count, own_count, cosine, sine, forward, backward):
    n1 = len(slabs)
    seg_len = n1 * LANES
    window = seg_len * seg_count
    rows = seg_count * own_count

    def over_window(value):
        total = value[:own_count]
        for g in range(1, seg_count):
            total = total + value[g * own_count : (g + 1) * own_count]
        return jnp.sum(total, axis=1, keepdims=True)

    def every_segment(value):
        return jnp.concatenate([value] * seg_count, axis=0)

    first = real_dft(slabs)
    turned = []
    for k, (re, im) in enumerate(first):
        if k:
            c, s = cosine[k : k + 1], sine[k : k + 1]
            re, im = re * c - im * s, re * s + im * c
        turned.append(jnp.concatenate([re, im], axis=1).astype(jnp.bfloat16))
    spectrum = jnp.dot(
        jnp.concatenate(turned, axis=0), forward, preferred_element_type=jnp.float32
    )
    parts, total = [], None
    for k in range(len(first)):
        re = spectrum[k * rows : (k + 1) * rows, :LANES]
        im = spectrum[k * rows : (k + 1) * rows, LANES:]
        magnitude = jnp.sqrt(re * re + im * im)
        parts.append((re, im, magnitude))
        term = magnitude if k in (0, n1 // 2) else 2.0 * magnitude
        total = term if total is None else total + term
    level = every_segment(WATER * over_window(total) / window + EPSILON)
    flat = []
    for re, im, magnitude in parts:
        inverse = 1.0 / (magnitude + level)
        flat.append(jnp.concatenate([re * inverse, im * inverse], axis=1).astype(jnp.bfloat16))
    back = jnp.dot(
        jnp.concatenate(flat, axis=0), backward, preferred_element_type=jnp.float32
    )
    turned = []
    for k in range(len(first)):
        re = back[k * rows : (k + 1) * rows, :LANES]
        im = back[k * rows : (k + 1) * rows, LANES:]
        if k:
            c, s = cosine[k : k + 1], sine[k : k + 1]
            re, im = re * c + im * s, im * c - re * s
        turned.append((re, im))
    trace = [slab * (1.0 / seg_len) for slab in real_inverse(turned, n1)]
    squares = trace[0] * trace[0]
    for slab in trace[1:]:
        squares = squares + slab * slab
    scale = every_segment(lax.rsqrt(over_window(squares) / window + EPSILON))
    return [slab * scale for slab in trace]


def gather_kernel(
    n_sta,
    n_seg,
    records,
    owners,
    own,
    series,
    received,
    held,
    names,
    flat,
    seg_send,
    seg_recv,
    z_send,
    z_recv,
    y_send,
    y_recv,
):
    depth = n_sta // n_seg
    planes = n_seg
    own_count, seg_len = records.shape
    n1 = seg_len // LANES
    g, s = lax.axis_index("seg"), lax.axis_index("sta")
    z, y = s // depth, s % depth

    names[...] = jnp.zeros_like(names)
    names[: owners.shape[0], : owners.shape[1]] = owners[...].astype(jnp.float32)
    barrier = pltpu.get_barrier_semaphore()
    for d in range(1, n_seg):
        pl.semaphore_signal(barrier, inc=1, device_id={"seg": (g + d) % n_seg}, device_id_type=MESH)
    for d in range(1, depth):
        pl.semaphore_signal(
            barrier, inc=1, device_id={"sta": z * depth + (y + d) % depth}, device_id_type=MESH
        )

    @pl.when(z > 0)
    def _():
        pl.semaphore_signal(barrier, inc=1, device_id={"sta": s - depth}, device_id_type=MESH)

    @pl.when(z < planes - 1)
    def _():
        pl.semaphore_signal(barrier, inc=1, device_id={"sta": s + depth}, device_id_type=MESH)

    below, above = (z + planes - 1) // planes, (2 * planes - 2 - z) // planes
    pl.semaphore_wait(barrier, n_seg - 1 + depth - 1 + below + above)

    copies = []
    for d in range(1, n_seg):
        copy = pltpu.make_async_remote_copy(
            src_ref=records,
            dst_ref=held.at[g],
            send_sem=seg_send.at[d - 1],
            recv_sem=seg_recv.at[d - 1],
            device_id={"seg": (g + d) % n_seg},
            device_id_type=MESH,
        )
        copy.start()
        copies.append(copy)
    held[g] = records[...]
    made = make_tables(seg_len, (n1 // 2 + 8) // 8 * 8)
    for copy in copies:
        copy.wait()

    slabs = []
    for t in range(n1):
        slabs.append(
            jnp.concatenate(
                [held[j, :, t * LANES : (t + 1) * LANES].astype(jnp.float32) for j in range(n_seg)],
                axis=0,
            )
        )
    result = whiten(slabs, n_seg, own_count, *made)
    for t in range(n1):
        rounded = result[t].astype(jnp.bfloat16)
        for j in range(n_seg):
            own[j * n1 + t] = rounded[j * own_count : (j + 1) * own_count]
            flat[j * n1 + t] = rounded[j * own_count : (j + 1) * own_count].astype(jnp.float32)
    own[n_seg * n1] = names[...].astype(jnp.bfloat16)

    @pl.when(z == g)
    def _():
        received[y] = own[...]

    up = jnp.logical_and(z >= g, z < planes - 1)
    down = jnp.logical_and(z <= g, z > 0)

    def along_z(j, target):
        size = n1 + (1 if j == n_seg - 1 else 0)
        part = received.at[y, pl.ds(j * n1, size)]
        return pltpu.make_async_remote_copy(
            src_ref=part,
            dst_ref=part,
            send_sem=z_send.at[j],
            recv_sem=z_recv.at[j],
            device_id={"sta": target},
            device_id_type=MESH,
        )

    def along_z_up(j):
        return along_z(j, s + depth)

    def along_z_down(j):
        size = n1 + (1 if j == n_seg - 1 else 0)
        part = received.at[y, pl.ds(j * n1, size)]
        return pltpu.make_async_remote_copy(
            src_ref=part,
            dst_ref=part,
            send_sem=z_send.at[n_seg + j],
            recv_sem=z_recv.at[j],
            device_id={"sta": s - depth},
            device_id_type=MESH,
        )

    def along_y(j, d):
        size = n1 + (1 if j == n_seg - 1 else 0)
        part = received.at[y, pl.ds(j * n1, size)]
        return pltpu.make_async_remote_copy(
            src_ref=part,
            dst_ref=part,
            send_sem=y_send.at[d - 1, j],
            recv_sem=y_recv.at[d - 1, j],
            device_id={"sta": z * depth + (y + d) % depth},
            device_id_type=MESH,
        )

    def send(j):
        @pl.when(up)
        def _():
            along_z_up(j).start()

        @pl.when(down)
        def _():
            along_z_down(j).start()

        for d in range(1, depth):
            along_y(j, d).start()

    @pl.when(z == g)
    def _():
        for j in range(n_seg):
            send(j)

    edge = LAGS // 2 // LANES
    series[...] = jnp.zeros_like(series)
    for a in range(own_count):
        series[a, edge : edge + n_seg * n1] = flat[:, a, :]

    @pl.when(z != g)
    def _():
        for j in range(n_seg):
            along_z_up(j).wait_recv()
            send(j)

    for j in range(n_seg):
        for d in range(1, depth):
            along_y(j, d).wait()

        @pl.when(up)
        def _():
            along_z_up(j).wait_send()

        @pl.when(down)
        def _():
            along_z_down(j).wait_send()


def lag_kernel(n_sta, n_seg, slots, own, series, received, white, out, turned, shifted, rhs, rec, left, lhs, tails, grams, sums, order):
    depth = n_sta // n_seg
    nk, own_count = own.shape[0] - 1, own.shape[1]
    stations = depth * own_count
    parts = LANES // SUB
    tiles = LAGS // LANES
    per_tile = LANES // SUB
    me = lax.axis_index("sta").astype(jnp.float32)
    length = series.shape[1]

    g = lax.axis_index("seg")
    n1 = nk // n_seg
    for t in range(n1):
        white[:, t * LANES : (t + 1) * LANES] = own[g * n1 + t]

    for y in range(depth):
        rec[...] = received[y, :nk].astype(jnp.float32)
        for b in range(own_count):
            across = rec[:, b, :].T
            left[:, y * own_count + b, :] = jnp.concatenate(
                [across[c * SUB : (c + 1) * SUB] for c in range(parts)], axis=1
            )
    lhs[...] = left[...].reshape(SUB * stations, parts * nk).astype(jnp.bfloat16)

    lane = lax.broadcasted_iota(jnp.int32, (nk, LANES), 1)
    for first in range(0, own_count, per_tile):
        pieces = []
        for c in range(parts):
            piece = jnp.zeros((nk, LANES), jnp.float32)
            for q in range(per_tile):
                shift = (SUB * q - SUB * c - 1) % LANES
                moved = series[first + q, tiles : tiles + nk]
                moved = pltpu.roll(moved, shift, 1) if shift else moved
                piece = jnp.where(lane // SUB == q, moved, piece)
            pieces.append(piece)
        ends_of = jnp.dot(
            lhs[...],
            jnp.concatenate(pieces, axis=0).astype(jnp.bfloat16),
            preferred_element_type=jnp.float32,
        )
        place = lax.broadcasted_iota(jnp.int32, (stations, LANES), 1)
        added = jnp.zeros((stations, LANES), jnp.float32)
        for i in range(1, SUB):
            part = jnp.where(place % SUB < i, ends_of[i * stations : (i + 1) * stations], 0.0)
            added += pltpu.roll(part, SUB - i, 1)
        tails[first // per_tile] = added

    shape = (stations, stations)
    row = lax.broadcasted_iota(jnp.int32, shape, 0)
    station = lax.broadcasted_iota(jnp.int32, shape, 1)
    source, block = station // own_count, station % own_count // BS
    wide = (LANES, stations)
    number = lax.broadcasted_iota(jnp.int32, wide, 0)
    wide_station = lax.broadcasted_iota(jnp.int32, wide, 1)
    wide_block = wide_station % own_count // BS
    entry = lax.broadcasted_iota(jnp.int32, (own_count, LANES), 0)
    wanted = jnp.zeros(shape, jnp.float32)
    rank = jnp.zeros(shape, jnp.float32)
    for y in range(depth):
        names = received[y, nk].astype(jnp.float32)
        named = jnp.max(
            jnp.where(jnp.logical_and(entry < DESTS, names == me), 1.0, 0.0), axis=0, keepdims=True
        )
        named = jnp.broadcast_to(named, (stations, LANES)).astype(jnp.bfloat16)
        here = wide_station // own_count == y
        same = jnp.where(jnp.logical_and(here, number == wide_block), 1.0, 0.0)
        before = jnp.where(jnp.logical_and(here, number < wide_block), 1.0, 0.0)
        wanted += jnp.dot(named, same.astype(jnp.bfloat16), preferred_element_type=jnp.float32)
        rank += jnp.dot(named, before.astype(jnp.bfloat16), preferred_element_type=jnp.float32)
    slot = (row // BS % slots).astype(jnp.float32)
    hit = jnp.logical_and(row // (BS * slots) == source, row % BS == station % BS)
    hit = jnp.logical_and(hit, slot == rank)
    select = jnp.where(hit, wanted, 0.0).astype(jnp.bfloat16)
    rows = out.shape[0]
    window = nk * LANES
    scale = 1.0 / math.sqrt(window)
    lag_lane = lax.broadcasted_iota(jnp.int32, (stations, LANES), 1)
    last = lag_lane >= LANES - SUB
    whole_lane = lax.broadcasted_iota(jnp.int32, (length - 8, LANES), 1)

    def build(a, half, phases):
        whole = series[a]
        for c in phases:
            shift = LANES - SUB * c - 1
            moved = pltpu.roll(whole, shift, 1)
            turned[half, c] = moved
            shifted[half, c] = jnp.where(
                whole_lane < shift, moved[: length - 8], turned[half, c, 1 : length - 7]
            )
            for v in range(tiles):
                rhs[half, c * nk : (c + 1) * nk, v * LANES : (v + 1) * LANES] = shifted[
                    half, c, v : v + nk
                ].astype(jnp.bfloat16)

    def diagonal(half, low, size, first, count):
        if count == 1:
            start = first * stations + low
            term = grams[half, start : start + size]
            if not first:
                return term
            head = jnp.where(lag_lane[:size] < first, 0.0, term[:, :LANES])
            return jnp.concatenate([head, term[:, LANES:]], axis=1)
        count //= 2
        later = pltpu.roll(
            diagonal(half, low, size, first + count, count), LAGS - count, 1
        )
        return diagonal(half, low, size, first, count) + later

    def finish(a, slot_of, total):
        move = (LANES - SUB - SUB * (a % per_tile)) % LANES
        tail = pltpu.roll(tails[a // per_tile], move, 1)
        edge_tile = total[:, LAGS - LANES :] + jnp.where(last, tail, 0.0)
        total = jnp.concatenate([total[:, : LAGS - LANES], edge_tile], axis=1)
        sums[slot_of] = jnp.dot(
            select, (total * scale).astype(jnp.bfloat16), preferred_element_type=jnp.float32
        )[:rows]

    def one_step(a, half):
        other, following = 1 - half, jnp.minimum(a + 1, own_count - 1)
        previous = (a + own_count - 1) % own_count
        halves = []
        for n in range(2):
            columns = slice(n * LAGS // 2, (n + 1) * LAGS // 2)
            grams[half, :, columns] = jnp.dot(
                lhs[...], rhs[half, :, columns], preferred_element_type=jnp.float32
            )
            build(following, other, range(n * parts // 2, (n + 1) * parts // 2))
            halves.append(diagonal(other, n * stations // 2, stations // 2, 0, SUB))
        finish(previous, previous, jnp.concatenate(halves, axis=0))

    def pair(step, carry):
        one_step(2 * step, 0)
        one_step(2 * step + 1, 1)
        return carry

    grams[1] = jnp.zeros(grams.shape[1:], jnp.float32)
    build(0, 0, range(parts))
    lax.fori_loop(0, own_count // 2, pair, 0)
    finish(own_count - 1, own_count - 1, diagonal(1, 0, stations, 0, SUB))
    for a in range(own_count):
        order[:, a, :] = sums[a]
    square = (LAGS, LAGS)
    ends = lax.broadcasted_iota(jnp.int32, square, 0) + lax.broadcasted_iota(jnp.int32, square, 1)
    flip = jnp.where(ends == LAGS - 1, 1.0, 0.0).astype(jnp.bfloat16)
    out[...] = (
        jnp.dot(
            order[...].reshape(rows * own_count, LAGS).astype(jnp.bfloat16),
            flip,
            preferred_element_type=jnp.float32,
        )
        .astype(jnp.bfloat16)
        .reshape(rows, own_count, LAGS)
    )


def on_device(n_sta, n_seg, records, owners):
    own_count, seg_len = records.shape
    depth = n_sta // n_seg
    n1 = seg_len // LANES
    nk = n1 * n_seg
    length = (nk + LAGS // LANES + 7) // 8 * 8 + 8
    blocks = own_count // BS
    slots = max(2, 2 * blocks * DESTS // n_sta)
    vmem = pl.BlockSpec(memory_space=pltpu.VMEM)
    own, series, received = pl.pallas_call(
        functools.partial(gather_kernel, n_sta, n_seg),
        out_shape=(
            jax.ShapeDtypeStruct((nk + 1, own_count, LANES), jnp.bfloat16),
            jax.ShapeDtypeStruct((own_count, length, LANES), jnp.float32),
            jax.ShapeDtypeStruct((depth, nk + 1, own_count, LANES), jnp.bfloat16),
        ),
        in_specs=[vmem] * 2,
        out_specs=(vmem,) * 3,
        scratch_shapes=[
            pltpu.VMEM((n_seg, own_count, seg_len), jnp.bfloat16),
            pltpu.VMEM((own_count, LANES), jnp.float32),
            pltpu.VMEM((nk, own_count, LANES), jnp.float32),
            pltpu.SemaphoreType.DMA((n_seg - 1,)),
            pltpu.SemaphoreType.DMA((n_seg - 1,)),
            pltpu.SemaphoreType.DMA((2 * n_seg,)),
            pltpu.SemaphoreType.DMA((n_seg,)),
            pltpu.SemaphoreType.DMA((depth - 1, n_seg)),
            pltpu.SemaphoreType.DMA((depth - 1, n_seg)),
        ],
        compiler_params=pltpu.CompilerParams(
            collective_id=0, has_side_effects=True, vmem_limit_bytes=32 * 2**20
        ),
        name="whiten_and_gather",
    )(records, owners.T)
    stations = depth * own_count
    rows = depth * slots * BS
    parts = LANES // SUB
    white, correlations = pl.pallas_call(
        functools.partial(lag_kernel, n_sta, n_seg, slots),
        out_shape=(
            jax.ShapeDtypeStruct((own_count, seg_len), jnp.bfloat16),
            jax.ShapeDtypeStruct((rows, own_count, LAGS), jnp.bfloat16),
        ),
        in_specs=[vmem] * 3,
        out_specs=(vmem,) * 2,
        scratch_shapes=[
            pltpu.VMEM((2, parts, length, LANES), jnp.float32),
            pltpu.VMEM((2, parts, length - 8, LANES), jnp.float32),
            pltpu.VMEM((2, parts * nk, LAGS), jnp.bfloat16),
            pltpu.VMEM((nk, own_count, LANES), jnp.float32),
            pltpu.VMEM((SUB, stations, parts * nk), jnp.float32),
            pltpu.VMEM((SUB * stations, parts * nk), jnp.bfloat16),
            pltpu.VMEM((own_count * SUB // LANES, stations, LANES), jnp.float32),
            pltpu.VMEM((2, SUB * stations, LAGS), jnp.float32),
            pltpu.VMEM((own_count, rows, LAGS), jnp.float32),
            pltpu.VMEM((rows, own_count, LAGS), jnp.float32),
        ],
        compiler_params=pltpu.CompilerParams(vmem_limit_bytes=48 * 2**20),
        name="correlate",
    )(own, series, received)
    return white, correlations


def solution(mesh):
    return jax.shard_map(
        functools.partial(on_device, mesh.shape["sta"], mesh.shape["seg"]),
        mesh=mesh,
        in_specs=(P("sta", "seg"), P("sta", None)),
        out_specs=(P("sta", "seg"), P("seg", "sta", None)),
        check_vma=False,
    )
```

```python
import functools
import math

import jax
import jax.numpy as jnp
from jax import lax
from jax.experimental import pallas as pl
from jax.experimental.pallas import tpu as pltpu
from jax.sharding import PartitionSpec as P

LAGS = 512
LANES = 128
BS = 2
DESTS = 4
SUB = 16

WATER = 0.5
EPSILON = 1e-06
MESH = pl.DeviceIdType.MESH


def conj(value):
    return value[0], -value[1]


def real_dft(slabs):
    n = len(slabs)
    if n == 2:
        zero = jnp.zeros_like(slabs[0])
        return [(slabs[0] + slabs[1], zero), (slabs[0] - slabs[1], zero)]
    even, odd = real_dft(slabs[::2]), real_dft(slabs[1::2])
    half = n // 2

    def at(values, k):
        k %= half
        return values[k] if k <= half // 2 else conj(values[half - k])

    result = []
    for k in range(half + 1):
        c, s = math.cos(2 * math.pi * k / n), math.sin(2 * math.pi * k / n)
        (er, ei), (pr, pi) = at(even, k), at(odd, k)
        if k == 0:
            result.append((er + pr, ei + pi))
        elif k == half:
            result.append((er - pr, ei - pi))
        elif 4 * k == n:
            result.append((er - pi, ei + pr))
        else:
            result.append((er + c * pr - s * pi, ei + s * pr + c * pi))
    return result


def real_inverse(values, n):
    if n == 2:
        return [values[0][0] + values[1][0], values[0][0] - values[1][0]]
    half = n // 2
    even, odd = [], []
    for k in range(half // 2 + 1):
        (ar, ai), (br, bi) = values[k], conj(values[half - k])
        even.append((ar + br, ai + bi))
        dr, di = ar - br, ai - bi
        c, s = math.cos(2 * math.pi * k / n), math.sin(2 * math.pi * k / n)
        if k == 0:
            odd.append((dr, di))
        elif 4 * k == n:
            odd.append((di, -dr))
        else:
            odd.append((dr * c + di * s, di * c - dr * s))
    slabs = [None] * n
    slabs[::2] = real_inverse(even, half)
    slabs[1::2] = real_inverse(odd, half)
    return slabs


def make_tables(seg_len, count):
    shape = (LANES, LANES)
    row = lax.broadcasted_iota(jnp.int32, shape, 0)
    lane = lax.broadcasted_iota(jnp.int32, shape, 1)
    angle = (row * lane % LANES).astype(jnp.float32) * (2 * math.pi / LANES)
    c, s = jnp.cos(angle).astype(jnp.bfloat16), jnp.sin(angle).astype(jnp.bfloat16)
    forward = jnp.concatenate(
        [jnp.concatenate([c, s], axis=1), jnp.concatenate([-s, c], axis=1)], axis=0
    )
    backward = jnp.concatenate(
        [jnp.concatenate([c, -s], axis=1), jnp.concatenate([s, c], axis=1)], axis=0
    )
    turn = (row * lane)[:count].astype(jnp.float32) * (2 * math.pi / seg_len)
    return jnp.cos(turn), jnp.sin(turn), forward, backward


def whiten(slabs, seg_count, own_count, cosine, sine, forward, backward):
    n1 = len(slabs)
    seg_len = n1 * LANES
    window = seg_len * seg_count
    rows = seg_count * own_count

    def over_window(value):
        total = value[:own_count]
        for g in range(1, seg_count):
            total = total + value[g * own_count : (g + 1) * own_count]
        return jnp.sum(total, axis=1, keepdims=True)

    def every_segment(value):
        return jnp.concatenate([value] * seg_count, axis=0)

    first = real_dft(slabs)
    turned = []
    for k, (re, im) in enumerate(first):
        if k:
            c, s = cosine[k : k + 1], sine[k : k + 1]
            re, im = re * c - im * s, re * s + im * c
        turned.append(jnp.concatenate([re, im], axis=1).astype(jnp.bfloat16))
    spectrum = jnp.dot(
        jnp.concatenate(turned, axis=0), forward, preferred_element_type=jnp.float32
    )
    parts, total = [], None
    for k in range(len(first)):
        re = spectrum[k * rows : (k + 1) * rows, :LANES]
        im = spectrum[k * rows : (k + 1) * rows, LANES:]
        magnitude = jnp.sqrt(re * re + im * im)
        parts.append((re, im, magnitude))
        term = magnitude if k in (0, n1 // 2) else 2.0 * magnitude
        total = term if total is None else total + term
    level = every_segment(WATER * over_window(total) / window + EPSILON)
    flat = []
    for re, im, magnitude in parts:
        inverse = 1.0 / (magnitude + level)
        flat.append(jnp.concatenate([re * inverse, im * inverse], axis=1).astype(jnp.bfloat16))
    back = jnp.dot(
        jnp.concatenate(flat, axis=0), backward, preferred_element_type=jnp.float32
    )
    turned = []
    for k in range(len(first)):
        re = back[k * rows : (k + 1) * rows, :LANES]
        im = back[k * rows : (k + 1) * rows, LANES:]
        if k:
            c, s = cosine[k : k + 1], sine[k : k + 1]
            re, im = re * c + im * s, im * c - re * s
        turned.append((re, im))
    trace = [slab * (1.0 / seg_len) for slab in real_inverse(turned, n1)]
    squares = trace[0] * trace[0]
    for slab in trace[1:]:
        squares = squares + slab * slab
    scale = every_segment(lax.rsqrt(over_window(squares) / window + EPSILON))
    return [slab * scale for slab in trace]


def gather_kernel(
    n_sta,
    n_seg,
    records,
    owners,
    own,
    series,
    received,
    left,
    held,
    names,
    flat,
    seg_send,
    seg_recv,
    z_send,
    z_recv,
    y_send,
    y_recv,
):
    depth = n_sta // n_seg
    planes = n_seg
    own_count, seg_len = records.shape
    n1 = seg_len // LANES
    g, s = lax.axis_index("seg"), lax.axis_index("sta")
    z, y = s // depth, s % depth

    names[...] = jnp.zeros_like(names)
    names[: owners.shape[0], : owners.shape[1]] = owners[...].astype(jnp.float32)
    barrier = pltpu.get_barrier_semaphore()
    for d in range(1, n_seg):
        pl.semaphore_signal(barrier, inc=1, device_id={"seg": (g + d) % n_seg}, device_id_type=MESH)
    for d in range(1, depth):
        pl.semaphore_signal(
            barrier, inc=1, device_id={"sta": z * depth + (y + d) % depth}, device_id_type=MESH
        )

    @pl.when(z > 0)
    def _():
        pl.semaphore_signal(barrier, inc=1, device_id={"sta": s - depth}, device_id_type=MESH)

    @pl.when(z < planes - 1)
    def _():
        pl.semaphore_signal(barrier, inc=1, device_id={"sta": s + depth}, device_id_type=MESH)

    below, above = (z + planes - 1) // planes, (2 * planes - 2 - z) // planes
    pl.semaphore_wait(barrier, n_seg - 1 + depth - 1 + below + above)

    copies = []
    for d in range(1, n_seg):
        copy = pltpu.make_async_remote_copy(
            src_ref=records,
            dst_ref=held.at[g],
            send_sem=seg_send.at[d - 1],
            recv_sem=seg_recv.at[d - 1],
            device_id={"seg": (g + d) % n_seg},
            device_id_type=MESH,
        )
        copy.start()
        copies.append(copy)
    held[g] = records[...]
    made = make_tables(seg_len, (n1 // 2 + 8) // 8 * 8)
    for copy in copies:
        copy.wait()

    slabs = []
    for t in range(n1):
        slabs.append(
            jnp.concatenate(
                [held[j, :, t * LANES : (t + 1) * LANES].astype(jnp.float32) for j in range(n_seg)],
                axis=0,
            )
        )
    result = whiten(slabs, n_seg, own_count, *made)
    for t in range(n1):
        rounded = result[t].astype(jnp.bfloat16)
        for j in range(n_seg):
            own[j * n1 + t] = rounded[j * own_count : (j + 1) * own_count]
            flat[j * n1 + t] = rounded[j * own_count : (j + 1) * own_count].astype(jnp.float32)
    own[n_seg * n1] = names[...].astype(jnp.bfloat16)

    @pl.when(z == g)
    def _():
        received[y] = own[...]

    up = jnp.logical_and(z >= g, z < planes - 1)
    down = jnp.logical_and(z <= g, z > 0)

    def along_z(j, target):
        size = n1 + (1 if j == n_seg - 1 else 0)
        part = received.at[y, pl.ds(j * n1, size)]
        return pltpu.make_async_remote_copy(
            src_ref=part,
            dst_ref=part,
            send_sem=z_send.at[j],
            recv_sem=z_recv.at[j],
            device_id={"sta": target},
            device_id_type=MESH,
        )

    def along_z_up(j):
        return along_z(j, s + depth)

    def along_z_down(j):
        size = n1 + (1 if j == n_seg - 1 else 0)
        part = received.at[y, pl.ds(j * n1, size)]
        return pltpu.make_async_remote_copy(
            src_ref=part,
            dst_ref=part,
            send_sem=z_send.at[n_seg + j],
            recv_sem=z_recv.at[j],
            device_id={"sta": s - depth},
            device_id_type=MESH,
        )

    def along_y(j, d):
        size = n1 + (1 if j == n_seg - 1 else 0)
        part = received.at[y, pl.ds(j * n1, size)]
        return pltpu.make_async_remote_copy(
            src_ref=part,
            dst_ref=part,
            send_sem=y_send.at[d - 1, j],
            recv_sem=y_recv.at[d - 1, j],
            device_id={"sta": z * depth + (y + d) % depth},
            device_id_type=MESH,
        )

    def send(j):
        @pl.when(up)
        def _():
            along_z_up(j).start()

        @pl.when(down)
        def _():
            along_z_down(j).start()

        for d in range(1, depth):
            along_y(j, d).start()

    @pl.when(z == g)
    def _():
        for j in range(n_seg):
            send(j)

    edge = LAGS // 2 // LANES
    series[...] = jnp.zeros_like(series)
    for a in range(own_count):
        series[a, edge : edge + n_seg * n1] = flat[:, a, :]

    @pl.when(z != g)
    def _():
        for j in range(n_seg):
            along_z_up(j).wait_recv()
            send(j)

    def turn(source):
        flat[...] = received[source, : n_seg * n1].astype(jnp.float32)
        for b in range(own_count):
            across = flat[:, b, :].T
            left[source, :, b, :] = jnp.concatenate(
                [across[c * SUB : (c + 1) * SUB] for c in range(LANES // SUB)], axis=1
            )

    turn(y)
    for j in range(n_seg):
        for d in range(1, depth):
            along_y(j, d).wait()

        @pl.when(up)
        def _():
            along_z_up(j).wait_send()

        @pl.when(down)
        def _():
            along_z_down(j).wait_send()

    for d in range(1, depth):
        turn((y + d) % depth)


def lag_kernel(n_sta, n_seg, slots, own, series, received, left, white, out, turned, shifted, rhs, lhs, tails, grams, sums, order):
    depth = n_sta // n_seg
    nk, own_count = own.shape[0] - 1, own.shape[1]
    stations = depth * own_count
    parts = LANES // SUB
    tiles = LAGS // LANES
    per_tile = LANES // SUB
    me = lax.axis_index("sta").astype(jnp.float32)
    length = series.shape[1]

    g = lax.axis_index("seg")
    n1 = nk // n_seg
    for t in range(n1):
        white[:, t * LANES : (t + 1) * LANES] = own[g * n1 + t]

    for source in range(depth):
        lhs[:, source * own_count : (source + 1) * own_count, :] = left[source].astype(
            jnp.bfloat16
        )

    lane = lax.broadcasted_iota(jnp.int32, (nk, LANES), 1)
    for first in range(0, own_count, per_tile):
        pieces = []
        for c in range(parts):
            piece = jnp.zeros((nk, LANES), jnp.float32)
            for q in range(per_tile):
                shift = (SUB * q - SUB * c - 1) % LANES
                moved = series[first + q, tiles : tiles + nk]
                moved = pltpu.roll(moved, shift, 1) if shift else moved
                piece = jnp.where(lane // SUB == q, moved, piece)
            pieces.append(piece)
        ends_of = jnp.dot(
            lhs[...].reshape(SUB * stations, parts * nk),
            jnp.concatenate(pieces, axis=0).astype(jnp.bfloat16),
            preferred_element_type=jnp.float32,
        )
        place = lax.broadcasted_iota(jnp.int32, (stations, LANES), 1)
        added = jnp.zeros((stations, LANES), jnp.float32)
        for i in range(1, SUB):
            part = jnp.where(place % SUB < i, ends_of[i * stations : (i + 1) * stations], 0.0)
            added += pltpu.roll(part, SUB - i, 1)
        tails[first // per_tile] = added

    shape = (stations, stations)
    row = lax.broadcasted_iota(jnp.int32, shape, 0)
    station = lax.broadcasted_iota(jnp.int32, shape, 1)
    source, block = station // own_count, station % own_count // BS
    wide = (LANES, stations)
    number = lax.broadcasted_iota(jnp.int32, wide, 0)
    wide_station = lax.broadcasted_iota(jnp.int32, wide, 1)
    wide_block = wide_station % own_count // BS
    entry = lax.broadcasted_iota(jnp.int32, (own_count, LANES), 0)
    wanted = jnp.zeros(shape, jnp.float32)
    rank = jnp.zeros(shape, jnp.float32)
    for y in range(depth):
        names = received[y, nk].astype(jnp.float32)
        named = jnp.max(
            jnp.where(jnp.logical_and(entry < DESTS, names == me), 1.0, 0.0), axis=0, keepdims=True
        )
        named = jnp.broadcast_to(named, (stations, LANES)).astype(jnp.bfloat16)
        here = wide_station // own_count == y
        same = jnp.where(jnp.logical_and(here, number == wide_block), 1.0, 0.0)
        before = jnp.where(jnp.logical_and(here, number < wide_block), 1.0, 0.0)
        wanted += jnp.dot(named, same.astype(jnp.bfloat16), preferred_element_type=jnp.float32)
        rank += jnp.dot(named, before.astype(jnp.bfloat16), preferred_element_type=jnp.float32)
    slot = (row // BS % slots).astype(jnp.float32)
    hit = jnp.logical_and(row // (BS * slots) == source, row % BS == station % BS)
    hit = jnp.logical_and(hit, slot == rank)
    select = jnp.where(hit, wanted, 0.0).astype(jnp.bfloat16)
    rows = out.shape[0]
    window = nk * LANES
    scale = 1.0 / math.sqrt(window)
    lag_lane = lax.broadcasted_iota(jnp.int32, (stations, LANES), 1)
    last = lag_lane >= LANES - SUB
    whole_lane = lax.broadcasted_iota(jnp.int32, (length - 8, LANES), 1)

    def build(a, half, phases):
        whole = series[a]
        for c in phases:
            shift = LANES - SUB * c - 1
            moved = pltpu.roll(whole, shift, 1)
            turned[half, c] = moved
            shifted[half, c] = jnp.where(
                whole_lane < shift, moved[: length - 8], turned[half, c, 1 : length - 7]
            )
            for v in range(tiles):
                rhs[half, c * nk : (c + 1) * nk, v * LANES : (v + 1) * LANES] = shifted[
                    half, c, v : v + nk
                ].astype(jnp.bfloat16)

    def diagonal(half, low, size, first, count):
        if count == 1:
            start = first * stations + low
            term = grams[half, start : start + size]
            if not first:
                return term
            head = jnp.where(lag_lane[:size] < first, 0.0, term[:, :LANES])
            return jnp.concatenate([head, term[:, LANES:]], axis=1)
        count //= 2
        later = pltpu.roll(
            diagonal(half, low, size, first + count, count), LAGS - count, 1
        )
        return diagonal(half, low, size, first, count) + later

    def finish(a, slot_of, total):
        move = (LANES - SUB - SUB * (a % per_tile)) % LANES
        tail = pltpu.roll(tails[a // per_tile], move, 1)
        edge_tile = total[:, LAGS - LANES :] + jnp.where(last, tail, 0.0)
        total = jnp.concatenate([total[:, : LAGS - LANES], edge_tile], axis=1)
        sums[slot_of] = jnp.dot(
            select, (total * scale).astype(jnp.bfloat16), preferred_element_type=jnp.float32
        )[:rows]

    def one_step(a, half):
        other, following = 1 - half, jnp.minimum(a + 1, own_count - 1)
        previous = (a + own_count - 1) % own_count
        halves = []
        for n in range(2):
            columns = slice(n * LAGS // 2, (n + 1) * LAGS // 2)
            grams[half, :, columns] = jnp.dot(
                lhs[...].reshape(SUB * stations, parts * nk),
                rhs[half, :, columns],
                preferred_element_type=jnp.float32,
            )
            build(following, other, range(n * parts // 2, (n + 1) * parts // 2))
            halves.append(diagonal(other, n * stations // 2, stations // 2, 0, SUB))
        finish(previous, previous, jnp.concatenate(halves, axis=0))

    def pair(step, carry):
        one_step(2 * step, 0)
        one_step(2 * step + 1, 1)
        return carry

    grams[1] = jnp.zeros(grams.shape[1:], jnp.float32)
    build(0, 0, range(parts))
    lax.fori_loop(0, own_count // 2, pair, 0)
    finish(own_count - 1, own_count - 1, diagonal(1, 0, stations, 0, SUB))
    for a in range(own_count):
        order[:, a, :] = sums[a]
    square = (LAGS, LAGS)
    ends = lax.broadcasted_iota(jnp.int32, square, 0) + lax.broadcasted_iota(jnp.int32, square, 1)
    flip = jnp.where(ends == LAGS - 1, 1.0, 0.0).astype(jnp.bfloat16)
    out[...] = (
        jnp.dot(
            order[...].reshape(rows * own_count, LAGS).astype(jnp.bfloat16),
            flip,
            preferred_element_type=jnp.float32,
        )
        .astype(jnp.bfloat16)
        .reshape(rows, own_count, LAGS)
    )


def on_device(n_sta, n_seg, records, owners):
    own_count, seg_len = records.shape
    depth = n_sta // n_seg
    n1 = seg_len // LANES
    nk = n1 * n_seg
    length = (nk + LAGS // LANES + 7) // 8 * 8 + 8
    blocks = own_count // BS
    slots = max(2, 2 * blocks * DESTS // n_sta)
    vmem = pl.BlockSpec(memory_space=pltpu.VMEM)
    own, series, received, left = pl.pallas_call(
        functools.partial(gather_kernel, n_sta, n_seg),
        out_shape=(
            jax.ShapeDtypeStruct((nk + 1, own_count, LANES), jnp.bfloat16),
            jax.ShapeDtypeStruct((own_count, length, LANES), jnp.float32),
            jax.ShapeDtypeStruct((depth, nk + 1, own_count, LANES), jnp.bfloat16),
            jax.ShapeDtypeStruct((depth, SUB, own_count, LANES // SUB * nk), jnp.float32),
        ),
        in_specs=[vmem] * 2,
        out_specs=(vmem,) * 4,
        scratch_shapes=[
            pltpu.VMEM((n_seg, own_count, seg_len), jnp.bfloat16),
            pltpu.VMEM((own_count, LANES), jnp.float32),
            pltpu.VMEM((nk, own_count, LANES), jnp.float32),
            pltpu.SemaphoreType.DMA((n_seg - 1,)),
            pltpu.SemaphoreType.DMA((n_seg - 1,)),
            pltpu.SemaphoreType.DMA((2 * n_seg,)),
            pltpu.SemaphoreType.DMA((n_seg,)),
            pltpu.SemaphoreType.DMA((depth - 1, n_seg)),
            pltpu.SemaphoreType.DMA((depth - 1, n_seg)),
        ],
        compiler_params=pltpu.CompilerParams(
            collective_id=0, has_side_effects=True, vmem_limit_bytes=32 * 2**20
        ),
        name="whiten_and_gather",
    )(records, owners.T)
    stations = depth * own_count
    rows = depth * slots * BS
    parts = LANES // SUB
    white, correlations = pl.pallas_call(
        functools.partial(lag_kernel, n_sta, n_seg, slots),
        out_shape=(
            jax.ShapeDtypeStruct((own_count, seg_len), jnp.bfloat16),
            jax.ShapeDtypeStruct((rows, own_count, LAGS), jnp.bfloat16),
        ),
        in_specs=[vmem] * 4,
        out_specs=(vmem,) * 2,
        scratch_shapes=[
            pltpu.VMEM((2, parts, length, LANES), jnp.float32),
            pltpu.VMEM((2, parts, length - 8, LANES), jnp.float32),
            pltpu.VMEM((2, parts * nk, LAGS), jnp.bfloat16),
            pltpu.VMEM((SUB, stations, parts * nk), jnp.bfloat16),
            pltpu.VMEM((own_count * SUB // LANES, stations, LANES), jnp.float32),
            pltpu.VMEM((2, SUB * stations, LAGS), jnp.float32),
            pltpu.VMEM((own_count, rows, LAGS), jnp.float32),
            pltpu.VMEM((rows, own_count, LAGS), jnp.float32),
        ],
        compiler_params=pltpu.CompilerParams(vmem_limit_bytes=48 * 2**20),
        name="correlate",
    )(own, series, received, left)
    return white, correlations


def solution(mesh):
    return jax.shard_map(
        functools.partial(on_device, mesh.shape["sta"], mesh.shape["seg"]),
        mesh=mesh,
        in_specs=(P("sta", "seg"), P("sta", None)),
        out_specs=(P("sta", "seg"), P("seg", "sta", None)),
        check_vma=False,
    )
```

```python
import functools
import math

import jax
import jax.numpy as jnp
from jax import lax
from jax.experimental import pallas as pl
from jax.experimental.pallas import tpu as pltpu
from jax.sharding import PartitionSpec as P

LAGS = 512
LANES = 128
BS = 2
DESTS = 4
SUB = 16

WATER = 0.5
EPSILON = 1e-06
MESH = pl.DeviceIdType.MESH


def conj(value):
    return value[0], -value[1]


def real_dft(slabs):
    n = len(slabs)
    if n == 2:
        zero = jnp.zeros_like(slabs[0])
        return [(slabs[0] + slabs[1], zero), (slabs[0] - slabs[1], zero)]
    even, odd = real_dft(slabs[::2]), real_dft(slabs[1::2])
    half = n // 2

    def at(values, k):
        k %= half
        return values[k] if k <= half // 2 else conj(values[half - k])

    result = []
    for k in range(half + 1):
        c, s = math.cos(2 * math.pi * k / n), math.sin(2 * math.pi * k / n)
        (er, ei), (pr, pi) = at(even, k), at(odd, k)
        if k == 0:
            result.append((er + pr, ei + pi))
        elif k == half:
            result.append((er - pr, ei - pi))
        elif 4 * k == n:
            result.append((er - pi, ei + pr))
        else:
            result.append((er + c * pr - s * pi, ei + s * pr + c * pi))
    return result


def real_inverse(values, n):
    if n == 2:
        return [values[0][0] + values[1][0], values[0][0] - values[1][0]]
    half = n // 2
    even, odd = [], []
    for k in range(half // 2 + 1):
        (ar, ai), (br, bi) = values[k], conj(values[half - k])
        even.append((ar + br, ai + bi))
        dr, di = ar - br, ai - bi
        c, s = math.cos(2 * math.pi * k / n), math.sin(2 * math.pi * k / n)
        if k == 0:
            odd.append((dr, di))
        elif 4 * k == n:
            odd.append((di, -dr))
        else:
            odd.append((dr * c + di * s, di * c - dr * s))
    slabs = [None] * n
    slabs[::2] = real_inverse(even, half)
    slabs[1::2] = real_inverse(odd, half)
    return slabs


def make_tables(seg_len, count):
    shape = (LANES, LANES)
    row = lax.broadcasted_iota(jnp.int32, shape, 0)
    lane = lax.broadcasted_iota(jnp.int32, shape, 1)
    angle = (row * lane % LANES).astype(jnp.float32) * (2 * math.pi / LANES)
    c, s = jnp.cos(angle).astype(jnp.bfloat16), jnp.sin(angle).astype(jnp.bfloat16)
    forward = jnp.concatenate(
        [jnp.concatenate([c, s], axis=1), jnp.concatenate([-s, c], axis=1)], axis=0
    )
    backward = jnp.concatenate(
        [jnp.concatenate([c, -s], axis=1), jnp.concatenate([s, c], axis=1)], axis=0
    )
    turn = (row * lane)[:count].astype(jnp.float32) * (2 * math.pi / seg_len)
    return jnp.cos(turn), jnp.sin(turn), forward, backward


def whiten(slabs, seg_count, own_count, cosine, sine, forward, backward):
    n1 = len(slabs)
    seg_len = n1 * LANES
    window = seg_len * seg_count
    rows = seg_count * own_count

    def over_window(value):
        total = value[:own_count]
        for g in range(1, seg_count):
            total = total + value[g * own_count : (g + 1) * own_count]
        return jnp.sum(total, axis=1, keepdims=True)

    def every_segment(value):
        return jnp.concatenate([value] * seg_count, axis=0)

    first = real_dft(slabs)
    turned = []
    for k, (re, im) in enumerate(first):
        if k:
            c, s = cosine[k : k + 1], sine[k : k + 1]
            re, im = re * c - im * s, re * s + im * c
        turned.append(jnp.concatenate([re, im], axis=1).astype(jnp.bfloat16))
    spectrum = jnp.dot(
        jnp.concatenate(turned, axis=0), forward, preferred_element_type=jnp.float32
    )
    parts, total = [], None
    for k in range(len(first)):
        re = spectrum[k * rows : (k + 1) * rows, :LANES]
        im = spectrum[k * rows : (k + 1) * rows, LANES:]
        magnitude = jnp.sqrt(re * re + im * im)
        parts.append((re, im, magnitude))
        term = magnitude if k in (0, n1 // 2) else 2.0 * magnitude
        total = term if total is None else total + term
    level = every_segment(WATER * over_window(total) / window + EPSILON)
    flat = []
    for re, im, magnitude in parts:
        inverse = 1.0 / (magnitude + level)
        flat.append(jnp.concatenate([re * inverse, im * inverse], axis=1).astype(jnp.bfloat16))
    back = jnp.dot(
        jnp.concatenate(flat, axis=0), backward, preferred_element_type=jnp.float32
    )
    turned = []
    for k in range(len(first)):
        re = back[k * rows : (k + 1) * rows, :LANES]
        im = back[k * rows : (k + 1) * rows, LANES:]
        if k:
            c, s = cosine[k : k + 1], sine[k : k + 1]
            re, im = re * c + im * s, im * c - re * s
        turned.append((re, im))
    trace = [slab * (1.0 / seg_len) for slab in real_inverse(turned, n1)]
    squares = trace[0] * trace[0]
    for slab in trace[1:]:
        squares = squares + slab * slab
    scale = every_segment(lax.rsqrt(over_window(squares) / window + EPSILON))
    return [slab * scale for slab in trace]


def gather_kernel(
    n_sta,
    n_seg,
    records,
    owners,
    own,
    series,
    received,
    left,
    held,
    names,
    flat,
    seg_send,
    seg_recv,
    z_send,
    z_recv,
    y_send,
    y_recv,
):
    depth = n_sta // n_seg
    planes = n_seg
    own_count, seg_len = records.shape
    n1 = seg_len // LANES
    g, s = lax.axis_index("seg"), lax.axis_index("sta")
    z, y = s // depth, s % depth

    names[...] = jnp.zeros_like(names)
    names[: owners.shape[0], : owners.shape[1]] = owners[...].astype(jnp.float32)
    barrier = pltpu.get_barrier_semaphore()
    for d in range(1, n_seg):
        pl.semaphore_signal(barrier, inc=1, device_id={"seg": (g + d) % n_seg}, device_id_type=MESH)
    for d in range(1, depth):
        pl.semaphore_signal(
            barrier, inc=1, device_id={"sta": z * depth + (y + d) % depth}, device_id_type=MESH
        )

    @pl.when(z > 0)
    def _():
        pl.semaphore_signal(barrier, inc=1, device_id={"sta": s - depth}, device_id_type=MESH)

    @pl.when(z < planes - 1)
    def _():
        pl.semaphore_signal(barrier, inc=1, device_id={"sta": s + depth}, device_id_type=MESH)

    below, above = (z + planes - 1) // planes, (2 * planes - 2 - z) // planes
    pl.semaphore_wait(barrier, n_seg - 1 + depth - 1 + below + above)

    copies = []
    for d in range(1, n_seg):
        copy = pltpu.make_async_remote_copy(
            src_ref=records,
            dst_ref=held.at[g],
            send_sem=seg_send.at[d - 1],
            recv_sem=seg_recv.at[d - 1],
            device_id={"seg": (g + d) % n_seg},
            device_id_type=MESH,
        )
        copy.start()
        copies.append(copy)
    held[g] = records[...]
    made = make_tables(seg_len, (n1 // 2 + 8) // 8 * 8)
    for copy in copies:
        copy.wait()

    slabs = []
    for t in range(n1):
        slabs.append(
            jnp.concatenate(
                [held[j, :, t * LANES : (t + 1) * LANES].astype(jnp.float32) for j in range(n_seg)],
                axis=0,
            )
        )
    result = whiten(slabs, n_seg, own_count, *made)
    for t in range(n1):
        rounded = result[t].astype(jnp.bfloat16)
        for j in range(n_seg):
            own[j * n1 + t] = rounded[j * own_count : (j + 1) * own_count]
            flat[j * n1 + t] = rounded[j * own_count : (j + 1) * own_count].astype(jnp.float32)
    own[n_seg * n1] = names[...].astype(jnp.bfloat16)

    @pl.when(z == g)
    def _():
        received[y] = own[...]

    up = jnp.logical_and(z >= g, z < planes - 1)
    down = jnp.logical_and(z <= g, z > 0)

    def along_z(j, target):
        size = n1 + (1 if j == n_seg - 1 else 0)
        part = received.at[y, pl.ds(j * n1, size)]
        return pltpu.make_async_remote_copy(
            src_ref=part,
            dst_ref=part,
            send_sem=z_send.at[j],
            recv_sem=z_recv.at[j],
            device_id={"sta": target},
            device_id_type=MESH,
        )

    def along_z_up(j):
        return along_z(j, s + depth)

    def along_z_down(j):
        size = n1 + (1 if j == n_seg - 1 else 0)
        part = received.at[y, pl.ds(j * n1, size)]
        return pltpu.make_async_remote_copy(
            src_ref=part,
            dst_ref=part,
            send_sem=z_send.at[n_seg + j],
            recv_sem=z_recv.at[j],
            device_id={"sta": s - depth},
            device_id_type=MESH,
        )

    def along_y(j, d):
        size = n1 + (1 if j == n_seg - 1 else 0)
        part = received.at[y, pl.ds(j * n1, size)]
        return pltpu.make_async_remote_copy(
            src_ref=part,
            dst_ref=part,
            send_sem=y_send.at[d - 1, j],
            recv_sem=y_recv.at[d - 1, j],
            device_id={"sta": z * depth + (y + d) % depth},
            device_id_type=MESH,
        )

    def send(j):
        @pl.when(up)
        def _():
            along_z_up(j).start()

        @pl.when(down)
        def _():
            along_z_down(j).start()

        for d in range(1, depth):
            along_y(j, d).start()

    @pl.when(z == g)
    def _():
        for j in range(n_seg):
            send(j)

    edge = LAGS // 2 // LANES
    series[...] = jnp.zeros_like(series)
    for a in range(own_count):
        series[a, edge : edge + n_seg * n1] = flat[:, a, :]

    @pl.when(z != g)
    def _():
        for j in range(n_seg):
            along_z_up(j).wait_recv()
            send(j)

    def turn(source):
        flat[...] = received[source, : n_seg * n1].astype(jnp.float32)
        for b in range(own_count):
            across = flat[:, b, :].T
            left[source, :, b, :] = jnp.concatenate(
                [across[c * SUB : (c + 1) * SUB] for c in range(LANES // SUB)], axis=1
            )

    turn(y)
    for j in range(n_seg):
        for d in range(1, depth):
            along_y(j, d).wait()

        @pl.when(up)
        def _():
            along_z_up(j).wait_send()

        @pl.when(down)
        def _():
            along_z_down(j).wait_send()

    for d in range(1, depth):
        turn((y + d) % depth)


def lag_kernel(n_sta, n_seg, slots, own, series, received, left, white, out, turned, shifted, rhs, lhs, tails, grams, sums, order):
    depth = n_sta // n_seg
    nk, own_count = own.shape[0] - 1, own.shape[1]
    stations = depth * own_count
    parts = LANES // SUB
    tiles = LAGS // LANES
    per_tile = LANES // SUB
    me = lax.axis_index("sta").astype(jnp.float32)
    length = series.shape[1]

    g = lax.axis_index("seg")
    n1 = nk // n_seg
    for t in range(n1):
        white[:, t * LANES : (t + 1) * LANES] = own[g * n1 + t]

    for source in range(depth):
        lhs[:, source * own_count : (source + 1) * own_count, :] = left[source].astype(
            jnp.bfloat16
        )

    lane = lax.broadcasted_iota(jnp.int32, (nk, LANES), 1)
    for first in range(0, own_count, per_tile):
        pieces = []
        for c in range(parts):
            piece = jnp.zeros((nk, LANES), jnp.float32)
            for q in range(per_tile):
                shift = (SUB * q - SUB * c - 1) % LANES
                moved = series[first + q, tiles : tiles + nk]
                moved = pltpu.roll(moved, shift, 1) if shift else moved
                piece = jnp.where(lane // SUB == q, moved, piece)
            pieces.append(piece)
        ends_of = jnp.dot(
            lhs[...].reshape(SUB * stations, parts * nk),
            jnp.concatenate(pieces, axis=0).astype(jnp.bfloat16),
            preferred_element_type=jnp.float32,
        )
        place = lax.broadcasted_iota(jnp.int32, (stations, LANES), 1)
        added = jnp.zeros((stations, LANES), jnp.float32)
        for i in range(1, SUB):
            part = jnp.where(place % SUB < i, ends_of[i * stations : (i + 1) * stations], 0.0)
            added += pltpu.roll(part, SUB - i, 1)
        tails[first // per_tile] = added

    shape = (stations, stations)
    row = lax.broadcasted_iota(jnp.int32, shape, 0)
    station = lax.broadcasted_iota(jnp.int32, shape, 1)
    source, block = station // own_count, station % own_count // BS
    wide = (LANES, stations)
    number = lax.broadcasted_iota(jnp.int32, wide, 0)
    wide_station = lax.broadcasted_iota(jnp.int32, wide, 1)
    wide_block = wide_station % own_count // BS
    entry = lax.broadcasted_iota(jnp.int32, (own_count, LANES), 0)
    wanted = jnp.zeros(shape, jnp.float32)
    rank = jnp.zeros(shape, jnp.float32)
    for y in range(depth):
        names = received[y, nk].astype(jnp.float32)
        named = jnp.max(
            jnp.where(jnp.logical_and(entry < DESTS, names == me), 1.0, 0.0), axis=0, keepdims=True
        )
        named = jnp.broadcast_to(named, (stations, LANES)).astype(jnp.bfloat16)
        here = wide_station // own_count == y
        same = jnp.where(jnp.logical_and(here, number == wide_block), 1.0, 0.0)
        before = jnp.where(jnp.logical_and(here, number < wide_block), 1.0, 0.0)
        wanted += jnp.dot(named, same.astype(jnp.bfloat16), preferred_element_type=jnp.float32)
        rank += jnp.dot(named, before.astype(jnp.bfloat16), preferred_element_type=jnp.float32)
    slot = (row // BS % slots).astype(jnp.float32)
    hit = jnp.logical_and(row // (BS * slots) == source, row % BS == station % BS)
    hit = jnp.logical_and(hit, slot == rank)
    select = jnp.where(hit, wanted, 0.0).astype(jnp.bfloat16)
    rows = out.shape[0]
    window = nk * LANES
    scale = 1.0 / math.sqrt(window)
    lag_lane = lax.broadcasted_iota(jnp.int32, (stations, LANES), 1)
    last = lag_lane >= LANES - SUB
    whole_lane = lax.broadcasted_iota(jnp.int32, (length - 8, LANES), 1)

    def build(a, half, phases):
        whole = series[a]
        for c in phases:
            shift = LANES - SUB * c - 1
            moved = pltpu.roll(whole, shift, 1)
            turned[half, c] = moved
            shifted[half, c] = jnp.where(
                whole_lane < shift, moved[: length - 8], turned[half, c, 1 : length - 7]
            )
            for v in range(tiles):
                rhs[half, c * nk : (c + 1) * nk, v * LANES : (v + 1) * LANES] = shifted[
                    half, c, v : v + nk
                ].astype(jnp.bfloat16)

    def diagonal(half, low, size, first, count):
        if count == 1:
            start = first * stations + low
            term = grams[half, start : start + size]
            if not first:
                return term
            head = jnp.where(lag_lane[:size] < first, 0.0, term[:, :LANES])
            return jnp.concatenate([head, term[:, LANES:]], axis=1)
        count //= 2
        later = pltpu.roll(
            diagonal(half, low, size, first + count, count), LAGS - count, 1
        )
        return diagonal(half, low, size, first, count) + later

    def finish(a, slot_of, total):
        move = (LANES - SUB - SUB * (a % per_tile)) % LANES
        tail = pltpu.roll(tails[a // per_tile], move, 1)
        edge_tile = total[:, LAGS - LANES :] + jnp.where(last, tail, 0.0)
        total = jnp.concatenate([total[:, : LAGS - LANES], edge_tile], axis=1)
        sums[slot_of] = jnp.dot(
            select, (total * scale).astype(jnp.bfloat16), preferred_element_type=jnp.float32
        )[:rows]

    def one_step(a, half):
        other, following = 1 - half, jnp.minimum(a + 1, own_count - 1)
        previous = (a + own_count - 1) % own_count
        halves = []
        for n in range(2):
            columns = slice(n * LAGS // 2, (n + 1) * LAGS // 2)
            grams[half, :, columns] = jnp.dot(
                lhs[...].reshape(SUB * stations, parts * nk),
                rhs[half, :, columns],
                preferred_element_type=jnp.float32,
            )
            build(following, other, range(n * parts // 2, (n + 1) * parts // 2))
            halves.append(diagonal(other, n * stations // 2, stations // 2, 0, SUB))
        finish(previous, previous, jnp.concatenate(halves, axis=0))

    def four(step, carry):
        for k in range(4):
            one_step(4 * step + k, k % 2)
        return carry

    grams[1] = jnp.zeros(grams.shape[1:], jnp.float32)
    build(0, 0, range(parts))
    lax.fori_loop(0, own_count // 4, four, 0)
    finish(own_count - 1, own_count - 1, diagonal(1, 0, stations, 0, SUB))
    for a in range(own_count):
        order[:, a, :] = sums[a]
    square = (LAGS, LAGS)
    ends = lax.broadcasted_iota(jnp.int32, square, 0) + lax.broadcasted_iota(jnp.int32, square, 1)
    flip = jnp.where(ends == LAGS - 1, 1.0, 0.0).astype(jnp.bfloat16)
    out[...] = (
        jnp.dot(
            order[...].reshape(rows * own_count, LAGS).astype(jnp.bfloat16),
            flip,
            preferred_element_type=jnp.float32,
        )
        .astype(jnp.bfloat16)
        .reshape(rows, own_count, LAGS)
    )


def on_device(n_sta, n_seg, records, owners):
    own_count, seg_len = records.shape
    depth = n_sta // n_seg
    n1 = seg_len // LANES
    nk = n1 * n_seg
    length = (nk + LAGS // LANES + 7) // 8 * 8 + 8
    blocks = own_count // BS
    slots = max(2, 2 * blocks * DESTS // n_sta)
    vmem = pl.BlockSpec(memory_space=pltpu.VMEM)
    own, series, received, left = pl.pallas_call(
        functools.partial(gather_kernel, n_sta, n_seg),
        out_shape=(
            jax.ShapeDtypeStruct((nk + 1, own_count, LANES), jnp.bfloat16),
            jax.ShapeDtypeStruct((own_count, length, LANES), jnp.float32),
            jax.ShapeDtypeStruct((depth, nk + 1, own_count, LANES), jnp.bfloat16),
            jax.ShapeDtypeStruct((depth, SUB, own_count, LANES // SUB * nk), jnp.float32),
        ),
        in_specs=[vmem] * 2,
        out_specs=(vmem,) * 4,
        scratch_shapes=[
            pltpu.VMEM((n_seg, own_count, seg_len), jnp.bfloat16),
            pltpu.VMEM((own_count, LANES), jnp.float32),
            pltpu.VMEM((nk, own_count, LANES), jnp.float32),
            pltpu.SemaphoreType.DMA((n_seg - 1,)),
            pltpu.SemaphoreType.DMA((n_seg - 1,)),
            pltpu.SemaphoreType.DMA((2 * n_seg,)),
            pltpu.SemaphoreType.DMA((n_seg,)),
            pltpu.SemaphoreType.DMA((depth - 1, n_seg)),
            pltpu.SemaphoreType.DMA((depth - 1, n_seg)),
        ],
        compiler_params=pltpu.CompilerParams(
            collective_id=0, has_side_effects=True, vmem_limit_bytes=32 * 2**20
        ),
        name="whiten_and_gather",
    )(records, owners.T)
    stations = depth * own_count
    rows = depth * slots * BS
    parts = LANES // SUB
    white, correlations = pl.pallas_call(
        functools.partial(lag_kernel, n_sta, n_seg, slots),
        out_shape=(
            jax.ShapeDtypeStruct((own_count, seg_len), jnp.bfloat16),
            jax.ShapeDtypeStruct((rows, own_count, LAGS), jnp.bfloat16),
        ),
        in_specs=[vmem] * 4,
        out_specs=(vmem,) * 2,
        scratch_shapes=[
            pltpu.VMEM((2, parts, length, LANES), jnp.float32),
            pltpu.VMEM((2, parts, length - 8, LANES), jnp.float32),
            pltpu.VMEM((2, parts * nk, LAGS), jnp.bfloat16),
            pltpu.VMEM((SUB, stations, parts * nk), jnp.bfloat16),
            pltpu.VMEM((own_count * SUB // LANES, stations, LANES), jnp.float32),
            pltpu.VMEM((2, SUB * stations, LAGS), jnp.float32),
            pltpu.VMEM((own_count, rows, LAGS), jnp.float32),
            pltpu.VMEM((rows, own_count, LAGS), jnp.float32),
        ],
        compiler_params=pltpu.CompilerParams(vmem_limit_bytes=48 * 2**20),
        name="correlate",
    )(own, series, received, left)
    return white, correlations


def solution(mesh):
    return jax.shard_map(
        functools.partial(on_device, mesh.shape["sta"], mesh.shape["seg"]),
        mesh=mesh,
        in_specs=(P("sta", "seg"), P("sta", None)),
        out_specs=(P("sta", "seg"), P("seg", "sta", None)),
        check_vma=False,
    )
```
